256 devices in a mesh: rows: 128 (over x, z, y_lo, core), cols: 2 (over y_hi).
Axes of the slice: x: 4, y: 4 (y_hi: 2, y_lo: 2; y = y_hi * 2 + y_lo), z: 8, core: 2. Of those that a mesh axis runs over, the one named last changes fastest.
Arguments:
- latent: bfloat16 [4, 3072, 48], P(None, 'rows', 'cols'), may hold values from -6 to 6
- offsets: int32 [2], replicated, may hold values from 0 to 23, as said below
- timestep: int32 [1], replicated, may hold values from 0 to 999
- conv_in_weight: bfloat16 [3, 3, 4, 320], replicated, may hold values from -1 to 1
- conv_in_bias: float32 [320], replicated, may hold values from -3 to 3
- norm_one_gain: float32 [320], replicated, may hold values from 0.1 to 1.9
- norm_one_shift: float32 [320], replicated, may hold values from -3 to 3
- conv_one_weight: bfloat16 [3, 3, 320, 320], replicated, may hold values from -0.109375 to 0.109375
- conv_one_bias: float32 [320], replicated, may hold values from -4 to 4
- time_one_weight: bfloat16 [320, 1280], replicated, may hold values from -0.3125 to 0.3125
- time_one_bias: float32 [1280], replicated, may hold values from -3 to 3
- time_two_weight: bfloat16 [1280, 1280], replicated, may hold values from -0.15625 to 0.15625
- time_two_bias: float32 [1280], replicated, may hold values from -3 to 3
- time_proj_weight: bfloat16 [1280, 320], replicated, may hold values from -0.15625 to 0.15625
- time_proj_bias: float32 [320], replicated, may hold values from -4 to 4
- norm_two_gain: float32 [320], replicated, may hold values from 0.1 to 1.9
- norm_two_shift: float32 [320], replicated, may hold values from -3 to 3
- conv_two_weight: bfloat16 [3, 3, 320, 320], replicated, may hold values from -0.109375 to 0.109375
- conv_two_bias: float32 [320], replicated, may hold values from -3 to 3
Outputs:
- blended: float32 [3072, 48, 320], P('rows', 'cols')
The draws below stay inside these ranges and needn't reach their ends.
Inputs may be any that keep to these rules, and one draw needn't show every extreme that they name: The two offsets differ; one of them equals 23.
All inputs are finite; a program needn't handle non-finite values.
Results may differ from the reference program's by a relative error of at most 0.0028.
Values may be sent and summed in bfloat16 or wider, within the bound.
A program may use at most 64 MiB of HBM per device.

```python
import math
import jax
import jax.numpy as jnp
from jax import lax

C = 320
TEMB = 1280
LATC = 4
GROUPS = 32
STRIDE = 24
TAIL = 8
WIN = 32
H = 3072
W = 48


def draw_offsets(key, part):
    key = jax.random.fold_in(key, 7)
    other_key, side_key = jax.random.split(key)
    topmost = jnp.full((), STRIDE - 1, jnp.int32)
    other = jax.random.randint(other_key, (), 0, STRIDE - 1).astype(jnp.int32)
    side = jax.random.randint(side_key, (), 0, 2).astype(jnp.int32)
    row_shift = jnp.where(side == 0, topmost, other)
    col_shift = jnp.where(side == 0, other, topmost)
    return jnp.stack([row_shift, col_shift]).astype(jnp.int32)


def level_of(own_key, extent, cuts, smallest, top_value):
    level, own = 1.0, jax.random.fold_in(own_key, 6)
    for position, shards_of in cuts:
        heights = jnp.exp(jax.random.uniform(jax.random.fold_in(own, position), (shards_of,), jnp.float32, smallest / len(cuts), top_value / len(cuts)))
        level = level * jnp.repeat(heights, extent[position] // shards_of).reshape([-1 if axis == position else 1 for axis in range(len(extent))])
    return level


def gaussian(stream_key, extent, deviation, limit, cuts=(), kind=jnp.bfloat16):
    factor_of = level_of(stream_key, extent, cuts, -0.22, 0.18) if cuts else 1.0
    result = jax.random.normal(stream_key, extent, jnp.float32) * deviation * factor_of
    return jnp.minimum(jnp.maximum(result, -limit), limit).astype(kind)


def setup_inputs(seed: int = 0) -> dict:
    streams_of = jax.random.split(jax.random.key(seed), 20)
    latent = gaussian(streams_of[0], (LATC, H, W), 1.0, 6.0, ((1, 128), (2, 2)))
    offsets = draw_offsets(jax.random.fold_in(streams_of[19], 71), 0)
    timestep = jax.random.randint(streams_of[2], (1,), 0, 1000).astype(jnp.int32)
    conv_in_weight = gaussian(streams_of[3], (3, 3, LATC, C), (9 * LATC) ** -0.5, 1.0)
    conv_in_bias = gaussian(streams_of[4], (C,), 0.5, 3.0, (), jnp.float32)
    norm_one_gain = jnp.clip(1.0 + 0.18 * jax.random.normal(streams_of[5], (C,), jnp.float32), 0.1, 1.9)
    norm_one_shift = gaussian(streams_of[6], (C,), 0.5, 3.0, (), jnp.float32)
    conv_one_weight = gaussian(streams_of[7], (3, 3, C, C), (9 * C) ** -0.5, 0.109375)
    conv_one_bias = gaussian(streams_of[8], (C,), 1.0, 4.0, (), jnp.float32)
    time_one_weight = gaussian(streams_of[9], (C, TEMB), C ** -0.5, 0.3125)
    time_one_bias = gaussian(streams_of[10], (TEMB,), 0.5, 3.0, (), jnp.float32)
    time_two_weight = gaussian(streams_of[11], (TEMB, TEMB), TEMB ** -0.5, 0.15625)
    time_two_bias = gaussian(streams_of[12], (TEMB,), 0.5, 3.0, (), jnp.float32)
    time_proj_weight = gaussian(streams_of[13], (TEMB, C), TEMB ** -0.5, 0.15625)
    time_proj_bias = gaussian(streams_of[14], (C,), 1.0, 4.0, (), jnp.float32)
    norm_two_gain = jnp.clip(1.0 + 0.18 * jax.random.normal(streams_of[15], (C,), jnp.float32), 0.1, 1.9)
    norm_two_shift = gaussian(streams_of[16], (C,), 0.5, 3.0, (), jnp.float32)
    conv_two_weight = gaussian(streams_of[17], (3, 3, C, C), (9 * C) ** -0.5, 0.109375)
    conv_two_bias = gaussian(streams_of[18], (C,), 0.5, 3.0, (), jnp.float32)
    return {"latent": latent, "offsets": offsets, "timestep": timestep, "conv_in_weight": conv_in_weight, "conv_in_bias": conv_in_bias, "norm_one_gain": norm_one_gain, "norm_one_shift": norm_one_shift, "conv_one_weight": conv_one_weight, "conv_one_bias": conv_one_bias, "time_one_weight": time_one_weight, "time_one_bias": time_one_bias, "time_two_weight": time_two_weight, "time_two_bias": time_two_bias, "time_proj_weight": time_proj_weight, "time_proj_bias": time_proj_bias, "norm_two_gain": norm_two_gain, "norm_two_shift": norm_two_shift, "conv_two_weight": conv_two_weight, "conv_two_bias": conv_two_bias}


def time_vector(timestep, time_one_weight, time_one_bias, time_two_weight, time_two_bias, time_proj_weight, time_proj_bias):
    half = C // 2
    freqs = jnp.exp(-math.log(10000.0) * jnp.arange(half).astype(jnp.float32) / half)
    angles = timestep.astype(jnp.float32)[0] * freqs
    sinus = jnp.concatenate([jnp.cos(angles), jnp.sin(angles)])[None].astype(jnp.bfloat16)
    embed_one = jax.nn.silu(jnp.dot(sinus, time_one_weight, preferred_element_type=jnp.float32) + time_one_bias).astype(jnp.bfloat16)
    embed_two = jax.nn.silu(jnp.dot(embed_one, time_two_weight, preferred_element_type=jnp.float32) + time_two_bias).astype(jnp.bfloat16)
    return jnp.dot(embed_two, time_proj_weight, preferred_element_type=jnp.float32)[0] + time_proj_bias

def convolve(image, kernel):
    return lax.conv_general_dilated(image.astype(jnp.float32), kernel.astype(jnp.float32), (1, 1), 'SAME', dimension_numbers=('NHWC', 'HWIO', 'NHWC'), precision=lax.Precision.HIGHEST)

def group_norm(values, gain, shift):
    batch, height, width, chans = values.shape
    grouped = values.reshape(batch, height, width, GROUPS, chans // GROUPS)
    mean = lax.optimization_barrier(jnp.mean(grouped, axis=(1, 2, 4), keepdims=True))
    var = lax.optimization_barrier(jnp.mean((grouped - mean) ** 2, axis=(1, 2, 4), keepdims=True))
    normed = ((grouped - mean) / jnp.sqrt(var + 1e-05)).reshape(batch, height, width, chans)
    return normed * gain + shift

def block(windows, time_shift, conv_in_weight, conv_in_bias, norm_one_gain, norm_one_shift, conv_one_weight, conv_one_bias, norm_two_gain, norm_two_shift, conv_two_weight, conv_two_bias):
    start = (convolve(windows, conv_in_weight) + conv_in_bias).astype(jnp.bfloat16)
    act_one = jax.nn.silu(group_norm(start.astype(jnp.float32), norm_one_gain, norm_one_shift)).astype(jnp.bfloat16)
    inner = convolve(act_one, conv_one_weight) + conv_one_bias + time_shift
    act_two = jax.nn.silu(group_norm(inner, norm_two_gain, norm_two_shift)).astype(jnp.bfloat16)
    return convolve(act_two, conv_two_weight) + conv_two_bias + start.astype(jnp.float32)

def reference(latent, offsets, timestep, conv_in_weight, conv_in_bias, norm_one_gain, norm_one_shift, conv_one_weight, conv_one_bias, time_one_weight, time_one_bias, time_two_weight, time_two_bias, time_proj_weight, time_proj_bias, norm_two_gain, norm_two_shift, conv_two_weight, conv_two_bias):
    row_off = offsets[0]
    col_off = offsets[1]
    time_shift = time_vector(timestep, time_one_weight, time_one_bias, time_two_weight, time_two_bias, time_proj_weight, time_proj_bias)
    pixels = jnp.transpose(latent, (1, 2, 0))
    rolled = jnp.roll(pixels, (-row_off, -col_off), axis=(0, 1))
    extended = jnp.concatenate([rolled, rolled[:TAIL]], 0)
    extended = jnp.concatenate([extended, extended[:, :TAIL]], 1)
    height = H
    width = W
    count_cols = W // STRIDE

    def one_row(index):
        band = lax.dynamic_slice_in_dim(extended, index * STRIDE, WIN, 0)
        windows = jnp.stack([band[:, b * STRIDE:b * STRIDE + WIN] for b in range(count_cols)])
        outputs = block(windows, time_shift, conv_in_weight, conv_in_bias, norm_one_gain, norm_one_shift, conv_one_weight, conv_one_bias, norm_two_gain, norm_two_shift, conv_two_weight, conv_two_bias)
        strip = jnp.zeros((WIN, width + TAIL, C), jnp.float32)
        for b in range(count_cols):
            strip = strip.at[:, b * STRIDE:b * STRIDE + WIN].add(outputs[b])
        return strip[:, :width].at[:, :TAIL].add(strip[:, width:])
    stacks = lax.map(one_row, jnp.arange(height // STRIDE).astype(jnp.int32))
    main = stacks[:, :STRIDE].at[:, :TAIL].add(jnp.roll(stacks[:, STRIDE:], 1, axis=0))
    total = main.reshape(height, width, C)
    row_pos = jnp.arange(height).astype(jnp.int32)
    col_pos = jnp.arange(width).astype(jnp.int32)
    row_count = 1.0 + (row_pos % STRIDE < TAIL).astype(jnp.float32)
    col_count = 1.0 + (col_pos % STRIDE < TAIL).astype(jnp.float32)
    blended = total / (row_count[:, None] * col_count[None, :])[:, :, None]
    return jnp.roll(blended, (row_off, col_off), axis=(0, 1))
```

```python
import functools
import math

import jax
import jax.numpy as jnp
from jax import lax
from jax.experimental import pallas as pl
from jax.experimental.pallas import tpu as pltpu
from jax.sharding import PartitionSpec as P

C = 320
TEMB = 1280
LATC = 4
GROUPS = 32
STRIDE = 24
WIN = 32
HALF = C // 2
SIZE = C // GROUPS
MAIN = 256
REST = C - MAIN
DEPTH = 3 * C
CHUNKS = 4
ROWS = WIN // CHUNKS
PIX = ROWS * WIN
EPS = 1e-05
MESH = pl.DeviceIdType.MESH
F32 = jnp.float32
BF16 = jnp.bfloat16

PLANS = {
    "low": dict(lead=0, prev=0, next=16, first=(2, 3), then=(0, 1), front=8, back=8),
    "mid": dict(lead=1, prev=16, next=0, first=(0, 1), then=(2, 3), front=8, back=8),
    "high": dict(lead=1, prev=8, next=8, first=(0, 3), then=(1, 2), front=8, back=8),
    "any": dict(lead=1, prev=24, next=8, first=(0, 1, 2, 3), then=(), front=24, back=24),
}


def silu(value):
    half = 0.5 * value
    return half * jnp.tanh(half) + half


def iota(shape, dim):
    return lax.broadcasted_iota(jnp.int32, shape, dim)


def split3(value):
    top = value.astype(BF16).astype(F32)
    left = value - top
    mid = left.astype(BF16).astype(F32)
    return jnp.concatenate([top, mid, left - mid, jnp.zeros_like(value)], axis=0).astype(BF16)


def group_sum(value, groups):
    parts = jnp.dot(split3(value), groups, preferred_element_type=F32)
    return parts[0:8] + parts[8:16] + parts[16:24]


def body(
    plan,
    row_axis,
    offsets_ref,
    timestep_ref,
    latent_ref,
    conv_in_ref,
    vec_hbm,
    tvec_hbm,
    conv_one_hbm,
    conv_two_hbm,
    time_one_hbm,
    time_two_hbm,
    time_proj_hbm,
    out_ref,
    ext,
    vec,
    tvec,
    time_one,
    time_two,
    time_proj,
    w_one,
    w_two,
    tail_one,
    tail_two,
    w_in,
    onehot,
    edge,
    cover,
    groups,
    shift_vec,
    lat,
    start,
    act,
    inner,
    band,
    means,
    spreads,
    norm_one,
    norm_two,
    send_prev,
    send_next,
    from_prev,
    from_next,
    vec_sems,
    time_sems,
    w_sems,
    lat_send,
    lat_recv,
    out_send,
    out_recv,
):
    lead, n_prev, n_next, front = plan["lead"], plan["prev"], plan["next"], plan["front"]
    row, col = lax.axis_index("rows"), lax.axis_index("cols")
    after, before = lax.rem(row + 1, row_axis), lax.rem(row + row_axis - 1, row_axis)
    other = 1 - col
    row_off = offsets_ref[0]
    col_off = offsets_ref[1]

    barrier = pltpu.get_barrier_semaphore()
    friends = [(before, col), (before, other), (row, other), (after, col), (after, other)]
    for friend in friends:
        pl.semaphore_signal(barrier, inc=1, device_id=friend, device_id_type=MESH)

    small = [
        pltpu.make_async_copy(vec_hbm, vec, vec_sems.at[0]),
        pltpu.make_async_copy(tvec_hbm, tvec, vec_sems.at[1]),
        pltpu.make_async_copy(time_one_hbm, time_one, time_sems.at[0]),
        pltpu.make_async_copy(time_two_hbm, time_two, time_sems.at[1]),
        pltpu.make_async_copy(time_proj_hbm, time_proj, time_sems.at[2]),
    ]
    for copy in small:
        copy.start()

    def weight_copies(source, target, slot):
        copies = []
        for dy in range(3):
            for dx in range(3):
                copies.append(
                    pltpu.make_async_copy(
                        source.at[dy, dx, pl.ds(0, MAIN)],
                        target.at[dy, pl.ds(dx * MAIN, MAIN)],
                        w_sems.at[slot, dy * 6 + dx * 2],
                    )
                )
                copies.append(
                    pltpu.make_async_copy(
                        source.at[dy, dx, pl.ds(MAIN, REST)],
                        target.at[dy, pl.ds(3 * MAIN + dx * REST, REST)],
                        w_sems.at[slot, dy * 6 + dx * 2 + 1],
                    )
                )
        return copies

    copies_one = weight_copies(conv_one_hbm, w_one, 0)
    copies_two = weight_copies(conv_two_hbm, w_two, 1)

    own_at = 24 * lead
    blank = jnp.zeros((STRIDE, 8), F32)
    pieces = []
    for channel in range(LATC):
        pieces += [latent_ref[channel].astype(F32), blank]
    ext[0, own_at : own_at + STRIDE, :] = jnp.concatenate(pieces, axis=1)

    pl.semaphore_wait(barrier, len(friends))

    own = ext.at[0, pl.ds(own_at, STRIDE)]
    heads = 8 if lead else 16
    head = ext.at[0, pl.ds(own_at, heads)]
    moves = [
        (own, ext.at[1, pl.ds(own_at, STRIDE)], (row, other)),
        (head, ext.at[0, pl.ds(own_at + STRIDE, heads)], (before, col)),
        (head, ext.at[1, pl.ds(own_at + STRIDE, heads)], (before, other)),
    ]
    if lead:
        moves += [
            (own, ext.at[0, pl.ds(0, STRIDE)], (after, col)),
            (own, ext.at[1, pl.ds(0, STRIDE)], (after, other)),
        ]
    lat_copies = []
    for place, (source, target, device) in enumerate(moves):
        copy = pltpu.make_async_remote_copy(
            src_ref=source,
            dst_ref=target,
            send_sem=lat_send.at[place],
            recv_sem=lat_recv.at[place],
            device_id=device,
            device_id_type=MESH,
        )
        copy.start()
        lat_copies.append(copy)
    for copy in copies_one:
        copy.start()
    for copy in copies_two:
        copy.start()

    tap = iota((MAIN, 128), 1)
    from_lane = iota((MAIN, 128), 0)
    same = ((from_lane & 127) >> 5) == (tap & 3)
    pick = jnp.where(same & (tap < 9 * LATC), 1.0, 0.0).astype(BF16)
    first_g, second_g = iota((C, C), 0), iota((C, C), 1)
    low_g = second_g - lax.rem(second_g, SIZE)
    groups[...] = jnp.where((first_g >= low_g) & (first_g < low_g + SIZE), 1.0, 0.0).astype(BF16)
    w_in[...] = jnp.zeros_like(w_in)
    w_in[0 : 9 * LATC, :] = jnp.concatenate(
        [conv_in_ref[dy, dx].astype(F32) for dy in range(3) for dx in range(3)], axis=0
    ).astype(BF16)

    slot = iota((WIN, C), 0)
    slot_wide = iota((WIN, MAIN), 0)
    lane_wide = iota((WIN, MAIN), 1)
    lane_col = lane_wide & 31
    lane_at = jnp.where(lane_col < STRIDE, (lane_wide >> 7) * STRIDE + lane_col, -100)
    for window in range(2):
        begin = col_off - 24 * window
        place = (slot_wide - begin) & 31
        column = begin + place
        column = jnp.where(column < 0, column + 48, column)
        column = jnp.where(column >= 48, column - 48, column)
        onehot[window] = jnp.where(lane_at == column, 1.0, 0.0)
        place = (slot - begin) & 31
        edge[window, 0] = jnp.where(place > 0, 1.0, 0.0)
        edge[window, 1] = jnp.where(place < WIN - 1, 1.0, 0.0)
    cover[0] = jnp.where((slot >= col_off) & (slot < STRIDE), 1.0, 0.0)
    cover[1] = jnp.where((slot <= col_off + 7) & (slot < STRIDE), 1.0, 0.0)
    cover[2] = jnp.where((slot <= col_off - 17) & (slot < 8), 1.0, 0.0)
    for window in range(2):
        lat[window, 0] = jnp.zeros((WIN, 128), F32)
        lat[window, WIN + 1] = jnp.zeros((WIN, 128), F32)
        act[window, 0] = jnp.zeros((WIN, 4 * MAIN), BF16)
        act[window, WIN + 1] = jnp.zeros((WIN, 4 * MAIN), BF16)
    band[0:front] = jnp.zeros((front, STRIDE, C), F32)
    band[front + WIN :] = jnp.zeros((plan["back"], STRIDE, C), F32)

    for copy in small:
        copy.wait()
    freq = jnp.exp(-math.log(10000.0) * iota((8, HALF), 1).astype(F32) / HALF)
    angle = timestep_ref[0].astype(F32) * freq
    cosine = jnp.concatenate([jnp.cos(angle)] * 2, axis=0).astype(BF16)
    sine = jnp.concatenate([jnp.sin(angle)] * 2, axis=0).astype(BF16)
    hidden = jnp.dot(cosine, time_one[0:HALF, :], preferred_element_type=F32)
    hidden += jnp.dot(sine, time_one[HALF:C, :], preferred_element_type=F32)
    hidden = silu(hidden + tvec[0:1, :]).astype(BF16)
    hidden = jnp.dot(hidden, time_two[...], preferred_element_type=F32)
    hidden = silu(hidden + tvec[1:2, :]).astype(BF16)
    shift = lax.dot_general(
        hidden, time_proj[...], (((1,), (1,)), ((), ())), preferred_element_type=F32
    )
    shift_vec[...] = shift[0:8] + vec[4:5, :] + vec[3:4, :]

    for copy in lat_copies:
        copy.wait()

    def place_latent(step, _):
        window, chunk = step // CHUNKS, lax.rem(step, CHUNKS)
        chosen = onehot[window]
        lines = []
        for line in range(ROWS):
            at = row_off + chunk * ROWS + line
            left = ext[0, pl.ds(at, 1), :]
            right = ext[1, pl.ds(at, 1), :]
            lines.append((jnp.concatenate([left, right], axis=1) * chosen).astype(BF16))
        spread = jnp.concatenate(lines, axis=0)
        got = jnp.dot(spread, pick, preferred_element_type=F32)
        lat[window, pl.ds(1 + chunk * ROWS, ROWS)] = got.reshape(ROWS, WIN, 128)
        return 0

    lax.fori_loop(0, 2 * CHUNKS, place_latent, 0)

    lane = iota((1, WIN, 128), 2) >> 2
    lane_row = lane // 3
    lane_col = lane - 3 * lane_row

    def keep_moments(step, value):
        mean = jnp.sum(value, axis=0, keepdims=True) * (1.0 / PIX)
        diff = value - mean
        means[step] = jnp.broadcast_to(mean, (8, C))
        spreads[step] = jnp.broadcast_to(jnp.sum(diff * diff, axis=0, keepdims=True), (8, C))

    def norm_lines(target, gain, offset):
        mean = []
        for window in range(2):
            total = means[window * CHUNKS, 0:1]
            for chunk in range(1, CHUNKS):
                total = total + means[window * CHUNKS + chunk, 0:1]
            mean.append(total * (1.0 / CHUNKS))
        spare = jnp.zeros((6, C), F32)
        centre = group_sum(jnp.concatenate(mean + [spare], axis=0), groups[...]) * (1.0 / SIZE)
        variance = []
        for window in range(2):
            total = jnp.zeros((1, C), F32)
            for chunk in range(CHUNKS):
                step = window * CHUNKS + chunk
                diff = means[step, 0:1] - centre[window : window + 1]
                total = total + spreads[step, 0:1] * (1.0 / PIX) + diff * diff
            variance.append(total * (1.0 / CHUNKS))
        var = group_sum(jnp.concatenate(variance + [spare], axis=0), groups[...]) * (1.0 / SIZE)
        scale = 0.5 * gain / jnp.sqrt(var + EPS)
        move = 0.5 * offset - centre * scale
        for window in range(2):
            target[window, 0] = jnp.broadcast_to(scale[window : window + 1], (8, C))
            target[window, 1] = jnp.broadcast_to(move[window : window + 1], (8, C))

    def run_in(step, _):
        window, chunk = step // CHUNKS, lax.rem(step, CHUNKS)
        full = lat[window, pl.ds(chunk * ROWS, ROWS + 2)]
        less = pltpu.roll(full, 1, 1) * edge[window, 0, :, 0:128]
        more = pltpu.roll(full, WIN - 1, 1) * edge[window, 1, :, 0:128]
        wide = jnp.where(lane_col == 0, less, jnp.where(lane_col == 1, full, more))
        patch = jnp.where(
            lane_row == 0,
            wide[0:ROWS],
            jnp.where(lane_row == 1, wide[1 : ROWS + 1], wide[2 : ROWS + 2]),
        )
        patch = patch.reshape(PIX, 128).astype(BF16)
        value = jnp.dot(patch, w_in[...], preferred_element_type=F32) + vec[0:1, :]
        value = value.astype(BF16)
        start[window, pl.ds(chunk * ROWS, ROWS)] = value.reshape(ROWS, WIN, C)
        keep_moments(step, value.astype(F32))
        return 0

    lax.fori_loop(0, 2 * CHUNKS, run_in, 0)
    norm_lines(norm_one, vec[1:2, :], vec[2:3, :])

    def three_columns(value, window):
        less = pltpu.roll(value, 1, 1) * edge[window, 0]
        more = pltpu.roll(value, WIN - 1, 1) * edge[window, 1]
        return less, value, more

    def store_act(window, chunk, parts):
        at = pl.ds(1 + chunk * ROWS, ROWS)
        for place, part in enumerate(parts):
            act[window, at, :, place * MAIN : (place + 1) * MAIN] = part[:, :, 0:MAIN].astype(BF16)
        rest = jnp.concatenate([part[:, :, MAIN:C] for part in parts], axis=2)
        act[window, at, :, 3 * MAIN : DEPTH] = rest.astype(BF16)

    def activate(value, lines, window):
        half = value * lines[window, 0, 0:1] + lines[window, 1, 0:1]
        return half * jnp.tanh(half) + half

    def run_act(step, _):
        window, chunk = step // CHUNKS, lax.rem(step, CHUNKS)
        value = start[window, pl.ds(chunk * ROWS, ROWS)].astype(F32)
        value = activate(value, norm_one, window)
        store_act(window, chunk, three_columns(value, window))
        return 0

    lax.fori_loop(0, 2 * CHUNKS, run_act, 0)

    def tails(weights, target):
        blocks = [weights[dy, :, MAIN:C] for dy in range(3)]
        target[...] = jnp.concatenate(blocks, axis=1)

    def convolve(window, chunk, weights, tail):
        wide = act[window, pl.ds(chunk * ROWS, ROWS + 2), :, 0:DEPTH]
        wide = wide.reshape((ROWS + 2) * WIN, DEPTH)
        total = jnp.dot(wide[0:PIX], weights[0, :, 0:MAIN], preferred_element_type=F32)
        total += jnp.dot(wide[WIN : WIN + PIX], weights[1, :, 0:MAIN], preferred_element_type=F32)
        total += jnp.dot(wide[2 * WIN :], weights[2, :, 0:MAIN], preferred_element_type=F32)
        rest = jnp.dot(wide, tail[...], preferred_element_type=F32)
        left = (
            rest[0:PIX, 0:REST]
            + rest[WIN : WIN + PIX, REST : 2 * REST]
            + rest[2 * WIN :, 2 * REST : 3 * REST]
        )
        return jnp.concatenate([total, left], axis=1)

    for copy in copies_one:
        copy.wait()
    tails(w_one, tail_one)

    def run_one(step, _):
        window, chunk = step // CHUNKS, lax.rem(step, CHUNKS)
        value = convolve(window, chunk, w_one, tail_one) + shift_vec[0:1, :]
        inner[window, pl.ds(chunk * ROWS, ROWS)] = value.reshape(ROWS, WIN, C)
        keep_moments(step, value)
        return 0

    lax.fori_loop(0, 2 * CHUNKS, run_one, 0)
    norm_lines(norm_two, vec[5:6, :], vec[6:7, :])

    def merge(first, second):
        main = first * cover[0] + second * cover[1]
        wrap = first[:, 16:24] * cover[2, 0:8]
        return jnp.concatenate([main[:, 0:8] + wrap, main[:, 8:WIN]], axis=1)

    def run_merge(chunk, _):
        lines = []
        for window in range(2):
            value = inner[window, pl.ds(chunk * ROWS, ROWS)]
            value = activate(value, norm_two, window).astype(BF16).astype(F32)
            lines.append(three_columns(value, window))
        store_act(0, chunk, [merge(lines[0][place], lines[1][place]) for place in range(3)])
        return 0

    lax.fori_loop(0, CHUNKS, run_merge, 0)

    for copy in copies_two:
        copy.wait()
    tails(w_two, tail_two)
    counted = cover[0] + cover[1]
    counted = jnp.concatenate([counted[0:8] + cover[2, 0:8], counted[8:STRIDE]], axis=0)

    def run_two(chunk):
        value = convolve(0, chunk, w_two, tail_two).reshape(ROWS, WIN, C)
        at = pl.ds(chunk * ROWS, ROWS)
        first, second = start[0, at].astype(F32), start[1, at].astype(F32)
        value = (value + merge(first, second))[:, 0:STRIDE] + counted * vec[7:8, :]
        band[pl.ds(front + chunk * ROWS, ROWS)] = value

    def run_chunks(chunks):
        if len(chunks) == 0:
            return
        step = chunks[1] - chunks[0]

        def one(index, _):
            run_two(chunks[0] + index * step)
            return 0

        lax.fori_loop(0, len(chunks), one, 0)

    run_chunks(plan["first"])

    def stage(target, base, count):
        def one(pair, _):
            upper = band[base + 2 * pair]
            lower = band[base + 2 * pair + 1]
            target[pair] = jnp.concatenate([upper, lower], axis=0).astype(BF16)
            return 0

        lax.fori_loop(0, count // 2, one, 0)

    out_copies = []
    if n_prev:
        stage(send_prev, front + 24 * lead - row_off - n_prev, n_prev)
        out_copies.append((send_prev, from_next, (before, col), 0))
    if n_next:
        stage(send_next, front + 24 + 24 * lead - row_off, n_next)
        out_copies.append((send_next, from_prev, (after, col), 1))
    started = []
    for source, target, device, place in out_copies:
        copy = pltpu.make_async_remote_copy(
            src_ref=source,
            dst_ref=target,
            send_sem=out_send.at[place],
            recv_sem=out_recv.at[place],
            device_id=device,
            device_id_type=MESH,
        )
        copy.start()
        started.append(copy)

    run_chunks(plan["then"])
    for copy in started:
        copy.wait()

    scale_cols = 1.0 / counted

    def finish(pair, has_prev, has_next):
        pieces = []
        for line in range(2):
            at = 2 * pair + line
            pieces.append(band[front + 24 * lead - row_off + at])
        value = jnp.concatenate(pieces, axis=0)
        if has_prev:
            value = value + from_prev[pair].astype(F32)
        if has_next:
            value = value + from_next[pair - (STRIDE - n_prev) // 2].astype(F32)
        for line in range(2):
            at = 2 * pair + line
            twice = lax.rem(at - row_off + 24, 24) < 8
            scale = jnp.where(twice, 0.5, 1.0)
            out_ref[at] = value[line * STRIDE : (line + 1) * STRIDE] * (scale_cols * scale)

    marks = sorted({0, n_next // 2, (STRIDE - n_prev) // 2, STRIDE // 2})
    for low, high in zip(marks[:-1], marks[1:]):
        has_prev = low < n_next // 2
        has_next = low >= (STRIDE - n_prev) // 2

        def one(pair, _, has_prev=has_prev, has_next=has_next):
            finish(pair, has_prev, has_next)
            return 0

        lax.fori_loop(low, high, one, 0)


def block_kernel(name, row_axis, ident, operands):
    plan = PLANS[name]
    hbm = pl.BlockSpec(memory_space=pl.ANY)
    smem = pl.BlockSpec(memory_space=pltpu.SMEM)
    vmem = pl.BlockSpec(memory_space=pltpu.VMEM)
    n_prev, n_next = max(plan["prev"], 2), max(plan["next"], 2)
    ext_rows = 56 if plan["lead"] else 40
    band_rows = plan["front"] + WIN + plan["back"]
    scratch = [
        pltpu.VMEM((2, ext_rows, 128), F32),
        pltpu.VMEM((8, C), F32),
        pltpu.VMEM((2, TEMB), F32),
        pltpu.VMEM((C, TEMB), BF16),
        pltpu.VMEM((TEMB, TEMB), BF16),
        pltpu.VMEM((C, TEMB), BF16),
        pltpu.VMEM((3, DEPTH, C), BF16),
        pltpu.VMEM((3, DEPTH, C), BF16),
        pltpu.VMEM((DEPTH, 3 * REST), BF16),
        pltpu.VMEM((DEPTH, 3 * REST), BF16),
        pltpu.VMEM((128, C), BF16),
        pltpu.VMEM((2, WIN, MAIN), F32),
        pltpu.VMEM((2, 2, WIN, C), F32),
        pltpu.VMEM((3, WIN, C), F32),
        pltpu.VMEM((C, C), BF16),
        pltpu.VMEM((8, C), F32),
        pltpu.VMEM((2, WIN + 2, WIN, 128), F32),
        pltpu.VMEM((2, WIN, WIN, C), BF16),
        pltpu.VMEM((2, WIN + 2, WIN, 4 * MAIN), BF16),
        pltpu.VMEM((2, WIN, WIN, C), F32),
        pltpu.VMEM((band_rows, STRIDE, C), F32),
        pltpu.VMEM((2 * CHUNKS, 8, C), F32),
        pltpu.VMEM((2 * CHUNKS, 8, C), F32),
        pltpu.VMEM((2, 2, 8, C), F32),
        pltpu.VMEM((2, 2, 8, C), F32),
        pltpu.VMEM((n_prev // 2, 2 * STRIDE, C), BF16),
        pltpu.VMEM((n_next // 2, 2 * STRIDE, C), BF16),
        pltpu.VMEM((n_next // 2, 2 * STRIDE, C), BF16),
        pltpu.VMEM((n_prev // 2, 2 * STRIDE, C), BF16),
        pltpu.SemaphoreType.DMA((2,)),
        pltpu.SemaphoreType.DMA((3,)),
        pltpu.SemaphoreType.DMA((2, 18)),
        pltpu.SemaphoreType.DMA((5,)),
        pltpu.SemaphoreType.DMA((5,)),
        pltpu.SemaphoreType.DMA((2,)),
        pltpu.SemaphoreType.DMA((2,)),
    ]
    return pl.pallas_call(
        functools.partial(body, plan, row_axis),
        out_shape=jax.ShapeDtypeStruct((STRIDE, STRIDE, C), F32),
        in_specs=[smem, smem, vmem, vmem] + [hbm] * 7,
        out_specs=vmem,
        scratch_shapes=scratch,
        compiler_params=pltpu.CompilerParams(
            collective_id=ident, has_side_effects=True, vmem_limit_bytes=56 * 1024 * 1024
        ),
        cost_estimate=pl.CostEstimate(
            flops=3 * 2 * 1024 * 2880 * 320, bytes_accessed=10**7, transcendentals=10**6
        ),
        name="panorama_block",
    )(*operands)


def on_device(
    row_axis,
    latent,
    offsets,
    timestep,
    conv_in_weight,
    conv_in_bias,
    norm_one_gain,
    norm_one_shift,
    conv_one_weight,
    conv_one_bias,
    time_one_weight,
    time_one_bias,
    time_two_weight,
    time_two_bias,
    time_proj_weight,
    time_proj_bias,
    norm_two_gain,
    norm_two_shift,
    conv_two_weight,
    conv_two_bias,
):
    vec = jnp.stack(
        [
            conv_in_bias,
            norm_one_gain,
            norm_one_shift,
            conv_one_bias,
            time_proj_bias,
            norm_two_gain,
            norm_two_shift,
            conv_two_bias,
        ]
    )
    tvec = jnp.stack([time_one_bias, time_two_bias])
    operands = (
        offsets,
        timestep,
        latent,
        conv_in_weight,
        vec,
        tvec,
        conv_one_weight,
        conv_two_weight,
        time_one_weight,
        time_two_weight,
        time_proj_weight.T,
    )
    return block_kernel("any", row_axis, 0, operands)


def solution(mesh):
    return jax.shard_map(
        functools.partial(on_device, mesh.shape["rows"]),
        mesh=mesh,
        in_specs=(P(None, "rows", "cols"),) + (P(),) * 18,
        out_specs=P("rows", "cols", None),
        check_vma=False,
    )
```

```python
import functools
import math

import jax
import jax.numpy as jnp
from jax import lax
from jax.experimental import pallas as pl
from jax.experimental.pallas import tpu as pltpu
from jax.sharding import PartitionSpec as P

C = 320
TEMB = 1280
LATC = 4
GROUPS = 32
STRIDE = 24
WIN = 32
HALF = C // 2
SIZE = C // GROUPS
MAIN = 256
REST = C - MAIN
DEPTH = 3 * C
CHUNKS = 4
ROWS = WIN // CHUNKS
EPS = 1e-05
AREA = WIN * WIN
MESH = pl.DeviceIdType.MESH
F32 = jnp.float32
BF16 = jnp.bfloat16

PLANS = {
    "low": dict(low=0, lead=0, prev=0, next=16, first=[(8, 8)], then=[(0, 8)], front=8, back=8),
    "mid": dict(low=8, lead=1, prev=16, next=0, first=[(0, 8)], then=[(8, 8)], front=8, back=8),
    "high": dict(
        low=16, lead=1, prev=8, next=8, first=[(0, 4), (12, 4)], then=[(4, 8)], front=8, back=8
    ),
}


def silu(value):
    half = 0.5 * value
    return half * jnp.tanh(half) + half


def iota(shape, dim):
    return lax.broadcasted_iota(jnp.int32, shape, dim)


def split3(value):
    top = value.astype(BF16).astype(F32)
    left = value - top
    mid = left.astype(BF16).astype(F32)
    return jnp.concatenate([top, mid, left - mid, jnp.zeros_like(value)], axis=0).astype(BF16)


def group_sum(value, groups):
    parts = jnp.dot(split3(value), groups, preferred_element_type=F32)
    return parts[0:8] + parts[8:16] + parts[16:24]


def body(
    plan,
    row_axis,
    offsets_hbm,
    timestep_hbm,
    latent_hbm,
    conv_in_hbm,
    conv_in_bias_hbm,
    gain_one_hbm,
    move_one_hbm,
    conv_one_bias_hbm,
    proj_bias_hbm,
    gain_two_hbm,
    move_two_hbm,
    conv_two_bias_hbm,
    time_one_bias_hbm,
    time_two_bias_hbm,
    conv_one_hbm,
    conv_two_hbm,
    time_one_hbm,
    time_two_hbm,
    time_proj_hbm,
    out_ref,
    offsets_ref,
    timestep_ref,
    latent_ref,
    conv_in_ref,
    ext,
    conv_in_bias,
    gain_one,
    move_one,
    conv_one_bias,
    proj_bias,
    gain_two,
    move_two,
    conv_two_bias,
    time_one_bias,
    time_two_bias,
    time_one,
    time_two,
    time_proj,
    w_one,
    w_two,
    tail_one,
    tail_two,
    w_in,
    onehot,
    edge,
    cover,
    wrap,
    groups,
    shift_vec,
    lat,
    start,
    act,
    inner,
    last,
    even,
    odd,
    band,
    means,
    spreads,
    norm_one,
    norm_two,
    send_prev,
    send_next,
    from_prev,
    from_next,
    in_sems,
    vec_sems,
    time_sems,
    w_sems,
    lat_send,
    lat_recv,
    out_send,
    out_recv,
):
    lead, n_prev, n_next, front = plan["lead"], plan["prev"], plan["next"], plan["front"]
    row, col = lax.axis_index("rows"), lax.axis_index("cols")
    after, before = lax.rem(row + 1, row_axis), lax.rem(row + row_axis - 1, row_axis)
    other = 1 - col
    barrier = pltpu.get_barrier_semaphore()
    friends = [(before, col), (before, other), (row, other), (after, col), (after, other)]
    for friend in friends:
        pl.semaphore_signal(barrier, inc=1, device_id=friend, device_id_type=MESH)

    arguments = [
        pltpu.make_async_copy(latent_hbm, latent_ref, in_sems.at[0]),
        pltpu.make_async_copy(offsets_hbm, offsets_ref, in_sems.at[1]),
        pltpu.make_async_copy(timestep_hbm, timestep_ref, in_sems.at[2]),
        pltpu.make_async_copy(conv_in_hbm, conv_in_ref, in_sems.at[3]),
    ]
    for copy in arguments:
        copy.start()
    small = [
        pltpu.make_async_copy(time_one_hbm, time_one, time_sems.at[0]),
        pltpu.make_async_copy(time_two_hbm, time_two, time_sems.at[1]),
        pltpu.make_async_copy(time_proj_hbm, time_proj, time_sems.at[2]),
    ]
    vectors = [
        (conv_in_bias_hbm, conv_in_bias),
        (gain_one_hbm, gain_one),
        (move_one_hbm, move_one),
        (conv_one_bias_hbm, conv_one_bias),
        (proj_bias_hbm, proj_bias),
        (gain_two_hbm, gain_two),
        (move_two_hbm, move_two),
        (conv_two_bias_hbm, conv_two_bias),
        (time_one_bias_hbm, time_one_bias),
        (time_two_bias_hbm, time_two_bias),
    ]
    for place, (source, target) in enumerate(vectors):
        small.append(pltpu.make_async_copy(source, target, vec_sems.at[place]))
    for copy in small:
        copy.start()

    def line_of(ref):
        return ref[...].reshape(1, ref.shape[0])

    def weight_copies(source, target, slot):
        copies = []
        for dy in range(3):
            for dx in range(3):
                copies.append(
                    pltpu.make_async_copy(
                        source.at[dy, dx, pl.ds(0, MAIN)],
                        target.at[dy, pl.ds(dx * MAIN, MAIN)],
                        w_sems.at[slot, dy * 6 + dx * 2],
                    )
                )
                copies.append(
                    pltpu.make_async_copy(
                        source.at[dy, dx, pl.ds(MAIN, REST)],
                        target.at[dy, pl.ds(3 * MAIN + dx * REST, REST)],
                        w_sems.at[slot, dy * 6 + dx * 2 + 1],
                    )
                )
        return copies

    copies_one = weight_copies(conv_one_hbm, w_one, 0)
    copies_two = weight_copies(conv_two_hbm, w_two, 1)

    for copy in arguments:
        copy.wait()
    row_off = jnp.clip(offsets_ref[0], plan["low"], plan["low"] + 7)
    col_off = offsets_ref[1]

    own_at = 24 * lead
    blank = jnp.zeros((STRIDE, 8), F32)
    pieces = []
    for channel in range(LATC):
        pieces += [latent_ref[channel].astype(F32), blank]
    ext[0, own_at : own_at + STRIDE, :] = jnp.concatenate(pieces, axis=1)

    pl.semaphore_wait(barrier, len(friends))

    own = ext.at[0, pl.ds(own_at, STRIDE)]
    heads = 8 if lead else 16
    head = ext.at[0, pl.ds(own_at, heads)]
    moves = [
        (own, ext.at[1, pl.ds(own_at, STRIDE)], (row, other)),
        (head, ext.at[0, pl.ds(own_at + STRIDE, heads)], (before, col)),
        (head, ext.at[1, pl.ds(own_at + STRIDE, heads)], (before, other)),
    ]
    if lead:
        moves += [
            (own, ext.at[0, pl.ds(0, STRIDE)], (after, col)),
            (own, ext.at[1, pl.ds(0, STRIDE)], (after, other)),
        ]
    lat_copies = []
    for place, (source, target, device) in enumerate(moves):
        copy = pltpu.make_async_remote_copy(
            src_ref=source,
            dst_ref=target,
            send_sem=lat_send.at[place],
            recv_sem=lat_recv.at[place],
            device_id=device,
            device_id_type=MESH,
        )
        copy.start()
        lat_copies.append(copy)
    for copy in copies_one:
        copy.start()
    for copy in copies_two:
        copy.start()

    tap = iota((MAIN, 128), 1)
    from_lane = iota((MAIN, 128), 0)
    same = ((from_lane & 127) >> 5) == (tap & 3)
    pick = jnp.where(same & (tap < 9 * LATC), 1.0, 0.0).astype(BF16)
    first_g, second_g = iota((C, C), 0), iota((C, C), 1)
    low_g = second_g - lax.rem(second_g, SIZE)
    groups[...] = jnp.where((first_g >= low_g) & (first_g < low_g + SIZE), 1.0, 0.0).astype(BF16)
    w_in[...] = jnp.zeros_like(w_in)
    w_in[0 : 9 * LATC, :] = jnp.concatenate(
        [conv_in_ref[dy, dx].astype(F32) for dy in range(3) for dx in range(3)], axis=0
    ).astype(BF16)

    slot = iota((WIN, C), 0)
    slot_wide = iota((WIN, MAIN), 0)
    lane_wide = iota((WIN, MAIN), 1)
    lane_col = lane_wide & 31
    lane_at = jnp.where(lane_col < STRIDE, (lane_wide >> 7) * STRIDE + lane_col, -100)
    for window in range(2):
        begin = col_off - 24 * window
        place = (slot_wide - begin) & 31
        column = begin + place
        column = jnp.where(column < 0, column + 48, column)
        column = jnp.where(column >= 48, column - 48, column)
        onehot[window] = jnp.where(lane_at == column, 1.0, 0.0)
        place = (slot - begin) & 31
        edge[window, 0] = jnp.where(place > 0, 1.0, 0.0)
        edge[window, 1] = jnp.where(place < WIN - 1, 1.0, 0.0)
    mine = iota((STRIDE, C), 0)
    near = iota((8, C), 0)
    for tap in range(3):
        for window in range(2):
            covered = (mine >= col_off) if window == 0 else (mine <= col_off + 7)
            mask = jnp.where(covered, 1.0, 0.0)
            if tap != 1:
                mask = mask * edge[window, tap // 2, 0:STRIDE]
            cover[window, tap] = mask
        mask = jnp.where(near <= col_off - 17, 1.0, 0.0)
        if tap != 1:
            mask = mask * edge[0, tap // 2, 16:24]
        wrap[tap] = mask
    for window in range(2):
        lat[window, 0] = jnp.zeros((WIN, 128), F32)
        lat[window, WIN + 1] = jnp.zeros((WIN, 128), F32)
        act[window, 0] = jnp.zeros((WIN, 4 * MAIN), BF16)
        act[window, WIN + 1] = jnp.zeros((WIN, 4 * MAIN), BF16)
    last[...] = jnp.zeros_like(last)
    band[0:front] = jnp.zeros((front, STRIDE, C), F32)
    band[front + WIN :] = jnp.zeros((plan["back"], STRIDE, C), F32)

    for copy in small:
        copy.wait()
    freq = jnp.exp(-math.log(10000.0) * iota((8, HALF), 1).astype(F32) / HALF)
    angle = timestep_ref[0].astype(F32) * freq
    cosine = jnp.concatenate([jnp.cos(angle)] * 2, axis=0).astype(BF16)
    sine = jnp.concatenate([jnp.sin(angle)] * 2, axis=0).astype(BF16)
    hidden = jnp.dot(cosine, time_one[0:HALF, :], preferred_element_type=F32)
    hidden += jnp.dot(sine, time_one[HALF:C, :], preferred_element_type=F32)
    hidden = silu(hidden + line_of(time_one_bias)).astype(BF16)
    hidden = jnp.dot(hidden, time_two[...], preferred_element_type=F32)
    hidden = silu(hidden + line_of(time_two_bias)).astype(BF16)
    shift = lax.dot_general(
        hidden, time_proj[...], (((1,), (1,)), ((), ())), preferred_element_type=F32
    )
    shift_vec[...] = shift[0:8] + line_of(proj_bias) + line_of(conv_one_bias)

    for copy in lat_copies:
        copy.wait_recv()

    lane = iota((1, WIN, 128), 2) >> 2
    lane_row = lane // 3
    lane_col = lane - 3 * lane_row

    def keep_moments(window, value):
        mean = jnp.sum(value, axis=0, keepdims=True) * (1.0 / AREA)
        diff = value - mean
        means[window] = jnp.broadcast_to(mean, (8, C))
        spread = jnp.sum(diff * diff, axis=0, keepdims=True) * (1.0 / AREA)
        spreads[window] = jnp.broadcast_to(spread, (8, C))

    def norm_lines(target, gain, offset):
        spare = jnp.zeros((6, C), F32)
        mean = jnp.concatenate([means[0, 0:1], means[1, 0:1], spare], axis=0)
        spread = jnp.concatenate([spreads[0, 0:1], spreads[1, 0:1], spare], axis=0)
        centre = group_sum(mean, groups[...]) * (1.0 / SIZE)
        diff = mean - centre
        var = group_sum(spread + diff * diff, groups[...]) * (1.0 / SIZE)
        scale = 0.5 * gain / jnp.sqrt(var + EPS)
        move = 0.5 * offset - centre * scale
        for window in range(2):
            target[window, 0] = jnp.broadcast_to(scale[window : window + 1], (8, C))
            target[window, 1] = jnp.broadcast_to(move[window : window + 1], (8, C))

    def run_in(window, _):
        chosen = onehot[window]
        lines = []
        for line in range(WIN):
            at = row_off + line
            left = ext[0, pl.ds(at, 1), :]
            right = ext[1, pl.ds(at, 1), :]
            lines.append((jnp.concatenate([left, right], axis=1) * chosen).astype(BF16))
        got = jnp.dot(jnp.concatenate(lines, axis=0), pick, preferred_element_type=F32)
        lat[window, 1 : WIN + 1] = got.reshape(WIN, WIN, 128)
        full = lat[window]
        less = pltpu.roll(full, 1, 1) * edge[window, 0, :, 0:128]
        more = pltpu.roll(full, WIN - 1, 1) * edge[window, 1, :, 0:128]
        wide = jnp.where(lane_col == 0, less, jnp.where(lane_col == 1, full, more))
        patch = jnp.where(
            lane_row == 0,
            wide[0:WIN],
            jnp.where(lane_row == 1, wide[1 : WIN + 1], wide[2 : WIN + 2]),
        )
        patch = patch.reshape(AREA, 128).astype(BF16)
        value = jnp.dot(patch, w_in[...], preferred_element_type=F32) + line_of(conv_in_bias)
        value = value.astype(BF16)
        start[window] = value.reshape(WIN, WIN, C)
        keep_moments(window, value.astype(F32))
        return 0

    lax.fori_loop(0, 2, run_in, 0)
    norm_lines(norm_one, line_of(gain_one), line_of(move_one))

    def three_columns(value, window):
        less = pltpu.roll(value, 1, 1) * edge[window, 0]
        more = pltpu.roll(value, WIN - 1, 1) * edge[window, 1]
        return less, value, more

    def rests(parts):
        return jnp.concatenate([part[..., MAIN:C] for part in parts], axis=-1).astype(BF16)

    def store_act(window, chunk, parts):
        at = pl.ds(1 + chunk * ROWS, ROWS)
        for place, part in enumerate(parts):
            act[window, at, :, place * MAIN : (place + 1) * MAIN] = part[:, :, 0:MAIN].astype(BF16)
        act[window, at, :, 3 * MAIN : DEPTH] = rests(parts)

    def activate(value, lines, window):
        half = value * lines[window, 0, 0:1] + lines[window, 1, 0:1]
        return half * jnp.tanh(half) + half

    def run_act(step, _):
        window, chunk = step // CHUNKS, lax.rem(step, CHUNKS)
        value = start[window, pl.ds(chunk * ROWS, ROWS)].astype(F32)
        value = activate(value, norm_one, window)
        store_act(window, chunk, three_columns(value, window))
        return 0

    lax.fori_loop(0, 2 * CHUNKS, run_act, 0)

    def tails(weights, target):
        blocks = [weights[dy, :, MAIN:C] for dy in range(3)]
        target[...] = jnp.concatenate(blocks, axis=1)

    def taps(sources, whole, width, weights, tail):
        pixels = sources[0].shape[0]
        total = jnp.dot(sources[0], weights[0, :, 0:MAIN], preferred_element_type=F32)
        total += jnp.dot(sources[1], weights[1, :, 0:MAIN], preferred_element_type=F32)
        total += jnp.dot(sources[2], weights[2, :, 0:MAIN], preferred_element_type=F32)
        rest = jnp.dot(whole, tail[...], preferred_element_type=F32)
        left = (
            rest[0:pixels, 0:REST]
            + rest[width : width + pixels, REST : 2 * REST]
            + rest[2 * width : 2 * width + pixels, 2 * REST : 3 * REST]
        )
        return jnp.concatenate([total, left], axis=1)

    for copy in copies_one:
        copy.wait()
    tails(w_one, tail_one)

    def run_one(window, _):
        sources = [act[window, dy : dy + WIN, :, 0:DEPTH].reshape(AREA, DEPTH) for dy in range(3)]
        whole = act[window, :, :, 0:DEPTH].reshape((WIN + 2) * WIN, DEPTH)
        value = taps(sources, whole, WIN, w_one, tail_one) + shift_vec[0:1, :]
        inner[window] = value.reshape(WIN, WIN, C)
        keep_moments(window, value)
        return 0

    lax.fori_loop(0, 2, run_one, 0)
    norm_lines(norm_two, line_of(gain_two), line_of(move_two))

    def merge(first, second, tap):
        main = first[:, 0:STRIDE] * cover[0, tap] + second[:, 0:STRIDE] * cover[1, tap]
        extra = first[:, 16:24] * wrap[tap]
        return jnp.concatenate([main[:, 0:8] + extra, main[:, 8:STRIDE]], axis=1)

    def store_pairs(target, at, count, parts):
        parts = [part.reshape(count, 2 * STRIDE, C) for part in parts]
        for place, part in enumerate(parts):
            target[at, :, place * MAIN : (place + 1) * MAIN] = part[:, :, 0:MAIN].astype(BF16)
        target[at, :, 3 * MAIN : DEPTH] = rests(parts)

    def run_merge(chunk, _):
        lines = []
        for window in range(2):
            value = inner[window, pl.ds(chunk * ROWS, ROWS)]
            value = activate(value, norm_two, window).astype(BF16).astype(F32)
            lines.append((pltpu.roll(value, 1, 1), value, pltpu.roll(value, WIN - 1, 1)))
        parts = [merge(lines[0][tap], lines[1][tap], tap) for tap in range(3)]
        at = pl.ds(chunk * (ROWS // 2), ROWS // 2)
        store_pairs(odd, at, ROWS // 2, parts)
        late = []
        for tap in range(3):
            late.append(jnp.concatenate([last[tap][None], parts[tap][0 : ROWS - 1]], axis=0))
            last[tap] = parts[tap][ROWS - 1]
        store_pairs(even, at, ROWS // 2, late)
        return 0

    lax.fori_loop(0, CHUNKS, run_merge, 0)
    nothing = jnp.zeros((1, STRIDE, C), F32)
    ends = [jnp.concatenate([last[tap][None], nothing], axis=0) for tap in range(3)]
    store_pairs(even, pl.ds(WIN // 2, 1), 1, ends)

    for copy in copies_two:
        copy.wait()
    tails(w_two, tail_two)
    counted = cover[0, 1] + cover[1, 1]
    counted = jnp.concatenate([counted[0:8] + wrap[1], counted[8:STRIDE]], axis=0)

    def run_two(pair, count):
        def flat(source, at, number):
            return source[at : at + number, :, 0:DEPTH].reshape(number * 2 * STRIDE, DEPTH)

        sources = [flat(even, pair, count), flat(odd, pair, count), flat(even, pair + 1, count)]
        value = taps(sources, flat(even, pair, count + 1), STRIDE, w_two, tail_two)
        value = value.reshape(2 * count, STRIDE, C)
        at = slice(2 * pair, 2 * pair + 2 * count)
        first, second = start[0, at].astype(F32), start[1, at].astype(F32)
        value = value + merge(first, second, 1) + counted * line_of(conv_two_bias)
        band[front + 2 * pair : front + 2 * pair + 2 * count] = value

    for pair, count in plan["first"]:
        run_two(pair, count)

    def stage(target, base, count):
        def one(pair, _):
            upper = band[base + 2 * pair]
            lower = band[base + 2 * pair + 1]
            target[pair] = jnp.concatenate([upper, lower], axis=0).astype(BF16)
            return 0

        lax.fori_loop(0, count // 2, one, 0)

    out_copies = []
    if n_prev:
        stage(send_prev, front + 24 * lead - row_off - n_prev, n_prev)
        out_copies.append((send_prev, from_next, (before, col), 0))
    if n_next:
        stage(send_next, front + 24 + 24 * lead - row_off, n_next)
        out_copies.append((send_next, from_prev, (after, col), 1))
    started = []
    for source, target, device, place in out_copies:
        copy = pltpu.make_async_remote_copy(
            src_ref=source,
            dst_ref=target,
            send_sem=out_send.at[place],
            recv_sem=out_recv.at[place],
            device_id=device,
            device_id_type=MESH,
        )
        copy.start()
        started.append(copy)

    for pair, count in plan["then"]:
        run_two(pair, count)
    for copy in started:
        copy.wait_recv()

    scale_cols = 1.0 / counted

    def finish(pair, has_prev, has_next):
        pieces = []
        for line in range(2):
            at = 2 * pair + line
            pieces.append(band[front + 24 * lead - row_off + at])
        value = jnp.concatenate(pieces, axis=0)
        if has_prev:
            value = value + from_prev[pair].astype(F32)
        if has_next:
            value = value + from_next[pair - (STRIDE - n_prev) // 2].astype(F32)
        for line in range(2):
            at = 2 * pair + line
            twice = lax.rem(at - row_off + 24, 24) < 8
            scale = jnp.where(twice, 0.5, 1.0)
            out_ref[at] = value[line * STRIDE : (line + 1) * STRIDE] * (scale_cols * scale)

    marks = sorted({0, n_next // 2, (STRIDE - n_prev) // 2, STRIDE // 2})
    for low, high in zip(marks[:-1], marks[1:]):
        has_prev = low < n_next // 2
        has_next = low >= (STRIDE - n_prev) // 2

        def one(pair, _, has_prev=has_prev, has_next=has_next):
            finish(pair, has_prev, has_next)
            return 0

        lax.fori_loop(low, high, one, 0)

    for copy in lat_copies + started:
        copy.wait_send()


def block_kernel(name, row_axis, ident, operands):
    plan = PLANS[name]
    hbm = pl.BlockSpec(memory_space=pl.ANY)
    vmem = pl.BlockSpec(memory_space=pltpu.VMEM)
    n_prev, n_next = max(plan["prev"], 2), max(plan["next"], 2)
    ext_rows = 56 if plan["lead"] else 40
    band_rows = plan["front"] + WIN + plan["back"]
    scratch = [
        pltpu.SMEM((2,), jnp.int32),
        pltpu.SMEM((1,), jnp.int32),
        pltpu.VMEM((LATC, STRIDE, STRIDE), BF16),
        pltpu.VMEM((3, 3, LATC, C), BF16),
        pltpu.VMEM((2, ext_rows, 128), F32),
    ]
    scratch += [pltpu.VMEM((C,), F32)] * 8 + [pltpu.VMEM((TEMB,), F32)] * 2
    scratch += [
        pltpu.VMEM((C, TEMB), BF16),
        pltpu.VMEM((TEMB, TEMB), BF16),
        pltpu.VMEM((C, TEMB), BF16),
        pltpu.VMEM((3, DEPTH, C), BF16),
        pltpu.VMEM((3, DEPTH, C), BF16),
        pltpu.VMEM((DEPTH, 3 * REST), BF16),
        pltpu.VMEM((DEPTH, 3 * REST), BF16),
        pltpu.VMEM((128, C), BF16),
        pltpu.VMEM((2, WIN, MAIN), F32),
        pltpu.VMEM((2, 2, WIN, C), F32),
        pltpu.VMEM((2, 3, STRIDE, C), F32),
        pltpu.VMEM((3, 8, C), F32),
        pltpu.VMEM((C, C), BF16),
        pltpu.VMEM((8, C), F32),
        pltpu.VMEM((2, WIN + 2, WIN, 128), F32),
        pltpu.VMEM((2, WIN, WIN, C), BF16),
        pltpu.VMEM((2, WIN + 2, WIN, 4 * MAIN), BF16),
        pltpu.VMEM((2, WIN, WIN, C), F32),
        pltpu.VMEM((3, STRIDE, C), F32),
        pltpu.VMEM((WIN // 2 + 1, 2 * STRIDE, 4 * MAIN), BF16),
        pltpu.VMEM((WIN // 2, 2 * STRIDE, 4 * MAIN), BF16),
        pltpu.VMEM((band_rows, STRIDE, C), F32),
        pltpu.VMEM((2, 8, C), F32),
        pltpu.VMEM((2, 8, C), F32),
        pltpu.VMEM((2, 2, 8, C), F32),
        pltpu.VMEM((2, 2, 8, C), F32),
        pltpu.VMEM((n_prev // 2, 2 * STRIDE, C), BF16),
        pltpu.VMEM((n_next // 2, 2 * STRIDE, C), BF16),
        pltpu.VMEM((n_next // 2, 2 * STRIDE, C), BF16),
        pltpu.VMEM((n_prev // 2, 2 * STRIDE, C), BF16),
        pltpu.SemaphoreType.DMA((4,)),
        pltpu.SemaphoreType.DMA((10,)),
        pltpu.SemaphoreType.DMA((3,)),
        pltpu.SemaphoreType.DMA((2, 18)),
        pltpu.SemaphoreType.DMA((5,)),
        pltpu.SemaphoreType.DMA((5,)),
        pltpu.SemaphoreType.DMA((2,)),
        pltpu.SemaphoreType.DMA((2,)),
    ]
    return pl.pallas_call(
        functools.partial(body, plan, row_axis),
        out_shape=jax.ShapeDtypeStruct((STRIDE, STRIDE, C), F32),
        in_specs=[hbm] * 19,
        out_specs=vmem,
        scratch_shapes=scratch,
        compiler_params=pltpu.CompilerParams(
            collective_id=ident, has_side_effects=True, vmem_limit_bytes=56 * 1024 * 1024
        ),
        cost_estimate=pl.CostEstimate(
            flops=3 * 2 * 1024 * 2880 * 320, bytes_accessed=10**7, transcendentals=10**6
        ),
        name="panorama_block",
    )(*operands)


def on_device(
    row_axis,
    latent,
    offsets,
    timestep,
    conv_in_weight,
    conv_in_bias,
    norm_one_gain,
    norm_one_shift,
    conv_one_weight,
    conv_one_bias,
    time_one_weight,
    time_one_bias,
    time_two_weight,
    time_two_bias,
    time_proj_weight,
    time_proj_bias,
    norm_two_gain,
    norm_two_shift,
    conv_two_weight,
    conv_two_bias,
):
    operands = (
        offsets,
        timestep,
        latent,
        conv_in_weight,
        conv_in_bias,
        norm_one_gain,
        norm_one_shift,
        conv_one_bias,
        time_proj_bias,
        norm_two_gain,
        norm_two_shift,
        conv_two_bias,
        time_one_bias,
        time_two_bias,
        conv_one_weight,
        conv_two_weight,
        time_one_weight,
        time_two_weight,
        time_proj_weight.T,
    )
    branches = [
        functools.partial(block_kernel, name, row_axis, place)
        for place, name in enumerate(("low", "mid", "high"))
    ]
    return lax.switch(offsets[0] >> 3, branches, operands)


def solution(mesh):
    return jax.shard_map(
        functools.partial(on_device, mesh.shape["rows"]),
        mesh=mesh,
        in_specs=(P(None, "rows", "cols"),) + (P(),) * 18,
        out_specs=P("rows", "cols", None),
        check_vma=False,
    )
```

```python
import functools
import math

import jax
import jax.numpy as jnp
from jax import lax
from jax.experimental import pallas as pl
from jax.experimental.pallas import tpu as pltpu
from jax.sharding import PartitionSpec as P

C = 320
TEMB = 1280
LATC = 4
GROUPS = 32
STRIDE = 24
WIN = 32
HALF = C // 2
SIZE = C // GROUPS
MAIN = 256
REST = C - MAIN
DEPTH = 3 * C
CHUNKS = 4
ROWS = WIN // CHUNKS
EPS = 1e-05
AREA = WIN * WIN
MESH = pl.DeviceIdType.MESH
F32 = jnp.float32
BF16 = jnp.bfloat16

PLANS = {
    "low": dict(low=0, lead=0, prev=0, next=16, first=[(8, 8)], then=[(0, 8)], front=8, back=8),
    "mid": dict(low=8, lead=1, prev=16, next=0, first=[(0, 8)], then=[(8, 8)], front=8, back=8),
    "high": dict(
        low=16, lead=1, prev=8, next=8, first=[(0, 4), (12, 4)], then=[(4, 8)], front=8, back=8
    ),
}


def silu(value):
    half = 0.5 * value
    return half * jnp.tanh(half) + half


def iota(shape, dim):
    return lax.broadcasted_iota(jnp.int32, shape, dim)


def split3(value):
    top = value.astype(BF16).astype(F32)
    left = value - top
    mid = left.astype(BF16).astype(F32)
    return jnp.concatenate([top, mid, left - mid, jnp.zeros_like(value)], axis=0).astype(BF16)


def group_sum(value, groups):
    parts = jnp.dot(split3(value), groups, preferred_element_type=F32)
    return parts[0:8] + parts[8:16] + parts[16:24]


def body(
    plan,
    row_axis,
    offsets_hbm,
    timestep_hbm,
    latent_hbm,
    conv_in_hbm,
    conv_in_bias_hbm,
    gain_one_hbm,
    move_one_hbm,
    conv_one_bias_hbm,
    proj_bias_hbm,
    gain_two_hbm,
    move_two_hbm,
    conv_two_bias_hbm,
    time_one_bias_hbm,
    time_two_bias_hbm,
    conv_one_hbm,
    conv_two_hbm,
    time_one_hbm,
    time_two_hbm,
    time_proj_hbm,
    out_ref,
    offsets_ref,
    timestep_ref,
    latent_ref,
    conv_in_ref,
    ext,
    conv_in_bias,
    gain_one,
    move_one,
    conv_one_bias,
    proj_bias,
    gain_two,
    move_two,
    conv_two_bias,
    time_one_bias,
    time_two_bias,
    time_one,
    time_two,
    time_proj,
    w_one,
    w_two,
    tail_one,
    tail_two,
    w_in,
    onehot,
    edge,
    cover,
    wrap,
    groups,
    shift_vec,
    lat,
    start,
    act,
    inner,
    last,
    even,
    odd,
    band,
    means,
    spreads,
    norm_one,
    norm_two,
    send_prev,
    send_next,
    from_prev,
    from_next,
    in_sems,
    vec_sems,
    time_sems,
    w_sems,
    lat_send,
    lat_recv,
    out_send,
    out_recv,
):
    lead, n_prev, n_next, front = plan["lead"], plan["prev"], plan["next"], plan["front"]
    row, col = lax.axis_index("rows"), lax.axis_index("cols")
    after, before = lax.rem(row + 1, row_axis), lax.rem(row + row_axis - 1, row_axis)
    other = 1 - col
    barrier = pltpu.get_barrier_semaphore()
    friends = [(before, col), (before, other), (row, other), (after, col), (after, other)]
    for friend in friends:
        pl.semaphore_signal(barrier, inc=1, device_id=friend, device_id_type=MESH)

    arguments = [
        pltpu.make_async_copy(latent_hbm, latent_ref, in_sems.at[0]),
        pltpu.make_async_copy(offsets_hbm, offsets_ref, in_sems.at[1]),
        pltpu.make_async_copy(timestep_hbm, timestep_ref, in_sems.at[2]),
        pltpu.make_async_copy(conv_in_hbm, conv_in_ref, in_sems.at[3]),
    ]
    for copy in arguments:
        copy.start()
    small = [
        pltpu.make_async_copy(time_one_hbm, time_one, time_sems.at[0]),
        pltpu.make_async_copy(time_two_hbm, time_two, time_sems.at[1]),
        pltpu.make_async_copy(time_proj_hbm, time_proj, time_sems.at[2]),
    ]
    vectors = [
        (conv_in_bias_hbm, conv_in_bias),
        (gain_one_hbm, gain_one),
        (move_one_hbm, move_one),
        (conv_one_bias_hbm, conv_one_bias),
        (proj_bias_hbm, proj_bias),
        (gain_two_hbm, gain_two),
        (move_two_hbm, move_two),
        (conv_two_bias_hbm, conv_two_bias),
        (time_one_bias_hbm, time_one_bias),
        (time_two_bias_hbm, time_two_bias),
    ]
    for place, (source, target) in enumerate(vectors):
        small.append(pltpu.make_async_copy(source, target, vec_sems.at[place]))
    for copy in small:
        copy.start()

    def line_of(ref):
        return ref[...].reshape(1, ref.shape[0])

    def weight_copies(source, target, slot):
        copies = []
        for dy in range(3):
            for dx in range(3):
                copies.append(
                    pltpu.make_async_copy(
                        source.at[dy, dx, pl.ds(0, MAIN)],
                        target.at[dy, pl.ds(dx * MAIN, MAIN)],
                        w_sems.at[slot, dy * 6 + dx * 2],
                    )
                )
                copies.append(
                    pltpu.make_async_copy(
                        source.at[dy, dx, pl.ds(MAIN, REST)],
                        target.at[dy, pl.ds(3 * MAIN + dx * REST, REST)],
                        w_sems.at[slot, dy * 6 + dx * 2 + 1],
                    )
                )
        return copies

    copies_one = weight_copies(conv_one_hbm, w_one, 0)
    copies_two = weight_copies(conv_two_hbm, w_two, 1)

    for copy in arguments:
        copy.wait()
    row_off = jnp.clip(offsets_ref[0], plan["low"], plan["low"] + 7)
    col_off = offsets_ref[1]

    own_at = 24 * lead
    blank = jnp.zeros((STRIDE, 8), F32)
    pieces = []
    for channel in range(LATC):
        pieces += [latent_ref[channel].astype(F32), blank]
    ext[0, own_at : own_at + STRIDE, :] = jnp.concatenate(pieces, axis=1)

    pl.semaphore_wait(barrier, len(friends))

    own = ext.at[0, pl.ds(own_at, STRIDE)]
    heads = 8 if lead else 16
    head = ext.at[0, pl.ds(own_at, heads)]
    moves = [
        (own, ext.at[1, pl.ds(own_at, STRIDE)], (row, other)),
        (head, ext.at[0, pl.ds(own_at + STRIDE, heads)], (before, col)),
        (head, ext.at[1, pl.ds(own_at + STRIDE, heads)], (before, other)),
    ]
    if lead:
        moves += [
            (own, ext.at[0, pl.ds(0, STRIDE)], (after, col)),
            (own, ext.at[1, pl.ds(0, STRIDE)], (after, other)),
        ]
    lat_copies = []
    for place, (source, target, device) in enumerate(moves):
        copy = pltpu.make_async_remote_copy(
            src_ref=source,
            dst_ref=target,
            send_sem=lat_send.at[place],
            recv_sem=lat_recv.at[place],
            device_id=device,
            device_id_type=MESH,
        )
        copy.start()
        lat_copies.append(copy)

    tap = iota((MAIN, 128), 1)
    from_lane = iota((MAIN, 128), 0)
    same = ((from_lane & 127) >> 5) == (tap & 3)
    pick = jnp.where(same & (tap < 9 * LATC), 1.0, 0.0).astype(BF16)
    first_g, second_g = iota((C, C), 0), iota((C, C), 1)
    low_g = second_g - lax.rem(second_g, SIZE)
    groups[...] = jnp.where((first_g >= low_g) & (first_g < low_g + SIZE), 1.0, 0.0).astype(BF16)
    w_in[...] = jnp.zeros_like(w_in)
    w_in[0 : 9 * LATC, :] = jnp.concatenate(
        [conv_in_ref[dy, dx].astype(F32) for dy in range(3) for dx in range(3)], axis=0
    ).astype(BF16)

    slot = iota((WIN, C), 0)
    slot_wide = iota((WIN, MAIN), 0)
    lane_wide = iota((WIN, MAIN), 1)
    lane_col = lane_wide & 31
    lane_at = jnp.where(lane_col < STRIDE, (lane_wide >> 7) * STRIDE + lane_col, -100)
    for window in range(2):
        begin = col_off - 24 * window
        place = (slot_wide - begin) & 31
        column = begin + place
        column = jnp.where(column < 0, column + 48, column)
        column = jnp.where(column >= 48, column - 48, column)
        onehot[window] = jnp.where(lane_at == column, 1.0, 0.0)
        place = (slot - begin) & 31
        edge[window, 0] = jnp.where(place > 0, 1.0, 0.0)
        edge[window, 1] = jnp.where(place < WIN - 1, 1.0, 0.0)
    mine = iota((STRIDE, C), 0)
    near = iota((8, C), 0)
    for tap in range(3):
        for window in range(2):
            covered = (mine >= col_off) if window == 0 else (mine <= col_off + 7)
            mask = jnp.where(covered, 1.0, 0.0)
            if tap != 1:
                mask = mask * edge[window, tap // 2, 0:STRIDE]
            cover[window, tap] = mask
        mask = jnp.where(near <= col_off - 17, 1.0, 0.0)
        if tap != 1:
            mask = mask * edge[0, tap // 2, 16:24]
        wrap[tap] = mask
    for window in range(2):
        lat[window, 0] = jnp.zeros((WIN, 128), F32)
        lat[window, WIN + 1] = jnp.zeros((WIN, 128), F32)
        act[window, 0] = jnp.zeros((WIN, 4 * MAIN), BF16)
        act[window, WIN + 1] = jnp.zeros((WIN, 4 * MAIN), BF16)
    last[...] = jnp.zeros_like(last)
    band[0:front] = jnp.zeros((front, STRIDE, C), F32)
    band[front + WIN :] = jnp.zeros((plan["back"], STRIDE, C), F32)

    for copy in small:
        copy.wait()
    for copy in copies_one:
        copy.start()
    freq = jnp.exp(-math.log(10000.0) * iota((8, HALF), 1).astype(F32) / HALF)
    angle = timestep_ref[0].astype(F32) * freq
    cosine = jnp.concatenate([jnp.cos(angle)] * 2, axis=0).astype(BF16)
    sine = jnp.concatenate([jnp.sin(angle)] * 2, axis=0).astype(BF16)
    hidden = jnp.dot(cosine, time_one[0:HALF, :], preferred_element_type=F32)
    hidden += jnp.dot(sine, time_one[HALF:C, :], preferred_element_type=F32)
    hidden = silu(hidden + line_of(time_one_bias)).astype(BF16)
    hidden = jnp.dot(hidden, time_two[...], preferred_element_type=F32)
    hidden = silu(hidden + line_of(time_two_bias)).astype(BF16)
    shift = lax.dot_general(
        hidden, time_proj[...], (((1,), (1,)), ((), ())), preferred_element_type=F32
    )
    shift_vec[...] = shift[0:8] + line_of(proj_bias) + line_of(conv_one_bias)

    for copy in lat_copies:
        copy.wait_recv()
    for copy in copies_two:
        copy.start()

    lane = iota((1, WIN, 128), 2) >> 2
    lane_row = lane // 3
    lane_col = lane - 3 * lane_row

    def fold(value):
        return jnp.sum(value.reshape(-1, 8, C), axis=0)

    def keep_moments(window, value):
        pivot = value[0:1]
        once = jnp.zeros((8, C), F32)
        twice = jnp.zeros((8, C), F32)
        for at in range(0, AREA, 256):
            diff = value[at : at + 256] - pivot
            once = once + fold(diff)
            twice = twice + fold(diff * diff)
        once = jnp.sum(once, axis=0, keepdims=True) * (1.0 / AREA)
        twice = jnp.sum(twice, axis=0, keepdims=True) * (1.0 / AREA)
        means[window] = jnp.broadcast_to(pivot + once, (8, C))
        spreads[window] = jnp.broadcast_to(jnp.maximum(twice - once * once, 0.0), (8, C))

    def norm_lines(target, gain, offset):
        spare = jnp.zeros((6, C), F32)
        mean = jnp.concatenate([means[0, 0:1], means[1, 0:1], spare], axis=0)
        spread = jnp.concatenate([spreads[0, 0:1], spreads[1, 0:1], spare], axis=0)
        centre = group_sum(mean, groups[...]) * (1.0 / SIZE)
        diff = mean - centre
        var = group_sum(spread + diff * diff, groups[...]) * (1.0 / SIZE)
        scale = 0.5 * gain / jnp.sqrt(var + EPS)
        move = 0.5 * offset - centre * scale
        for window in range(2):
            target[window, 0] = jnp.broadcast_to(scale[window : window + 1], (8, C))
            target[window, 1] = jnp.broadcast_to(move[window : window + 1], (8, C))

    def run_in(window, _):
        chosen = onehot[window]
        lines = []
        for line in range(WIN):
            at = row_off + line
            left = ext[0, pl.ds(at, 1), :]
            right = ext[1, pl.ds(at, 1), :]
            lines.append((jnp.concatenate([left, right], axis=1) * chosen).astype(BF16))
        got = jnp.dot(jnp.concatenate(lines, axis=0), pick, preferred_element_type=F32)
        lat[window, 1 : WIN + 1] = got.reshape(WIN, WIN, 128)
        full = lat[window]
        less = pltpu.roll(full, 1, 1) * edge[window, 0, :, 0:128]
        more = pltpu.roll(full, WIN - 1, 1) * edge[window, 1, :, 0:128]
        wide = jnp.where(lane_col == 0, less, jnp.where(lane_col == 1, full, more))
        patch = jnp.where(
            lane_row == 0,
            wide[0:WIN],
            jnp.where(lane_row == 1, wide[1 : WIN + 1], wide[2 : WIN + 2]),
        )
        patch = patch.reshape(AREA, 128).astype(BF16)
        value = jnp.dot(patch, w_in[...], preferred_element_type=F32) + line_of(conv_in_bias)
        value = value.astype(BF16)
        start[window] = value.reshape(WIN, WIN, C)
        keep_moments(window, value.astype(F32))
        return 0

    lax.fori_loop(0, 2, run_in, 0)
    norm_lines(norm_one, line_of(gain_one), line_of(move_one))

    def three_columns(value, window):
        less = pltpu.roll(value, 1, 1) * edge[window, 0]
        more = pltpu.roll(value, WIN - 1, 1) * edge[window, 1]
        return less, value, more

    def rests(parts):
        return jnp.concatenate([part[..., MAIN:C] for part in parts], axis=-1).astype(BF16)

    def store_act(window, chunk, parts):
        at = pl.ds(1 + chunk * ROWS, ROWS)
        for place, part in enumerate(parts):
            act[window, at, :, place * MAIN : (place + 1) * MAIN] = part[:, :, 0:MAIN].astype(BF16)
        act[window, at, :, 3 * MAIN : DEPTH] = rests(parts)

    def activate(value, lines, window):
        half = value * lines[window, 0, 0:1] + lines[window, 1, 0:1]
        return half * jnp.tanh(half) + half

    def run_act(step, _):
        window, chunk = step // CHUNKS, step % CHUNKS
        value = start[window, pl.ds(chunk * ROWS, ROWS)].astype(F32)
        value = activate(value, norm_one, window)
        store_act(window, chunk, three_columns(value, window))
        return 0

    lax.fori_loop(0, CHUNKS, run_act, 0)

    def tails(weights, target):
        blocks = [weights[dy, :, MAIN:C] for dy in range(3)]
        target[...] = jnp.concatenate(blocks, axis=1)

    def taps(sources, whole, width, weights, tail):
        pixels = sources[0].shape[0]
        total = jnp.dot(sources[0], weights[0, :, 0:MAIN], preferred_element_type=F32)
        total += jnp.dot(sources[1], weights[1, :, 0:MAIN], preferred_element_type=F32)
        total += jnp.dot(sources[2], weights[2, :, 0:MAIN], preferred_element_type=F32)
        rest = jnp.dot(whole, tail[...], preferred_element_type=F32)
        left = (
            rest[0:pixels, 0:REST]
            + rest[width : width + pixels, REST : 2 * REST]
            + rest[2 * width : 2 * width + pixels, 2 * REST : 3 * REST]
        )
        return jnp.concatenate([total, left], axis=1)

    for copy in copies_one:
        copy.wait()
    tails(w_one, tail_one)

    def run_one(window, _):
        sources = [act[window, dy : dy + WIN, :, 0:DEPTH].reshape(AREA, DEPTH) for dy in range(3)]
        whole = act[window, :, :, 0:DEPTH].reshape((WIN + 2) * WIN, DEPTH)
        value = taps(sources, whole, WIN, w_one, tail_one) + shift_vec[0:1, :]
        inner[window] = value.reshape(WIN, WIN, C)
        keep_moments(window, value)
        return 0

    for step in range(CHUNKS, 2 * CHUNKS):
        run_act(step, 0)
    run_one(0, 0)
    run_one(1, 0)
    norm_lines(norm_two, line_of(gain_two), line_of(move_two))

    def merge(first, second, tap):
        main = first[:, 0:STRIDE] * cover[0, tap] + second[:, 0:STRIDE] * cover[1, tap]
        extra = first[:, 16:24] * wrap[tap]
        return jnp.concatenate([main[:, 0:8] + extra, main[:, 8:STRIDE]], axis=1)

    def store_pairs(target, at, count, parts):
        parts = [part.reshape(count, 2 * STRIDE, C) for part in parts]
        for place, part in enumerate(parts):
            target[at, :, place * MAIN : (place + 1) * MAIN] = part[:, :, 0:MAIN].astype(BF16)
        target[at, :, 3 * MAIN : DEPTH] = rests(parts)

    def run_merge(chunk, _):
        lines = []
        for window in range(2):
            value = inner[window, pl.ds(chunk * ROWS, ROWS)]
            value = activate(value, norm_two, window).astype(BF16).astype(F32)
            lines.append((pltpu.roll(value, 1, 1), value, pltpu.roll(value, WIN - 1, 1)))
        parts = [merge(lines[0][tap], lines[1][tap], tap) for tap in range(3)]
        at = pl.ds(chunk * (ROWS // 2), ROWS // 2)
        store_pairs(odd, at, ROWS // 2, parts)
        late = []
        for tap in range(3):
            late.append(jnp.concatenate([last[tap][None], parts[tap][0 : ROWS - 1]], axis=0))
            last[tap] = parts[tap][ROWS - 1]
        store_pairs(even, at, ROWS // 2, late)
        return 0

    lax.fori_loop(0, CHUNKS, run_merge, 0)
    nothing = jnp.zeros((1, STRIDE, C), F32)
    ends = [jnp.concatenate([last[tap][None], nothing], axis=0) for tap in range(3)]
    store_pairs(even, pl.ds(WIN // 2, 1), 1, ends)

    for copy in copies_two:
        copy.wait()
    tails(w_two, tail_two)
    counted = cover[0, 1] + cover[1, 1]
    counted = jnp.concatenate([counted[0:8] + wrap[1], counted[8:STRIDE]], axis=0)

    def run_two(pair, count):
        def flat(source, at, number):
            return source[at : at + number, :, 0:DEPTH].reshape(number * 2 * STRIDE, DEPTH)

        sources = [flat(even, pair, count), flat(odd, pair, count), flat(even, pair + 1, count)]
        value = taps(sources, flat(even, pair, count + 1), STRIDE, w_two, tail_two)
        value = value.reshape(2 * count, STRIDE, C)
        at = slice(2 * pair, 2 * pair + 2 * count)
        first, second = start[0, at].astype(F32), start[1, at].astype(F32)
        value = value + merge(first, second, 1) + counted * line_of(conv_two_bias)
        band[front + 2 * pair : front + 2 * pair + 2 * count] = value

    for pair, count in plan["first"]:
        run_two(pair, count)

    def stage(target, base, count):
        def one(pair, _):
            upper = band[base + 2 * pair]
            lower = band[base + 2 * pair + 1]
            target[pair] = jnp.concatenate([upper, lower], axis=0).astype(BF16)
            return 0

        lax.fori_loop(0, count // 2, one, 0)

    out_copies = []
    if n_prev:
        stage(send_prev, front + 24 * lead - row_off - n_prev, n_prev)
        out_copies.append((send_prev, from_next, (before, col), 0))
    if n_next:
        stage(send_next, front + 24 + 24 * lead - row_off, n_next)
        out_copies.append((send_next, from_prev, (after, col), 1))
    started = []
    for source, target, device, place in out_copies:
        copy = pltpu.make_async_remote_copy(
            src_ref=source,
            dst_ref=target,
            send_sem=out_send.at[place],
            recv_sem=out_recv.at[place],
            device_id=device,
            device_id_type=MESH,
        )
        copy.start()
        started.append(copy)

    for pair, count in plan["then"]:
        run_two(pair, count)
    for copy in started:
        copy.wait_recv()

    scale_cols = 1.0 / counted

    def finish(pair, has_prev, has_next):
        pieces = []
        for line in range(2):
            at = 2 * pair + line
            pieces.append(band[front + 24 * lead - row_off + at])
        value = jnp.concatenate(pieces, axis=0)
        if has_prev:
            value = value + from_prev[pair].astype(F32)
        if has_next:
            value = value + from_next[pair - (STRIDE - n_prev) // 2].astype(F32)
        for line in range(2):
            at = 2 * pair + line
            twice = lax.rem(at - row_off + 24, 24) < 8
            scale = jnp.where(twice, 0.5, 1.0)
            out_ref[at] = value[line * STRIDE : (line + 1) * STRIDE] * (scale_cols * scale)

    marks = sorted({0, n_next // 2, (STRIDE - n_prev) // 2, STRIDE // 2})
    for low, high in zip(marks[:-1], marks[1:]):
        has_prev = low < n_next // 2
        has_next = low >= (STRIDE - n_prev) // 2

        def one(pair, _, has_prev=has_prev, has_next=has_next):
            finish(pair, has_prev, has_next)
            return 0

        lax.fori_loop(low, high, one, 0)

    for copy in lat_copies + started:
        copy.wait_send()


def block_kernel(name, row_axis, ident, operands):
    plan = PLANS[name]
    hbm = pl.BlockSpec(memory_space=pl.ANY)
    vmem = pl.BlockSpec(memory_space=pltpu.VMEM)
    n_prev, n_next = max(plan["prev"], 2), max(plan["next"], 2)
    ext_rows = 56 if plan["lead"] else 40
    band_rows = plan["front"] + WIN + plan["back"]
    scratch = [
        pltpu.SMEM((2,), jnp.int32),
        pltpu.SMEM((1,), jnp.int32),
        pltpu.VMEM((LATC, STRIDE, STRIDE), BF16),
        pltpu.VMEM((3, 3, LATC, C), BF16),
        pltpu.VMEM((2, ext_rows, 128), F32),
    ]
    scratch += [pltpu.VMEM((C,), F32)] * 8 + [pltpu.VMEM((TEMB,), F32)] * 2
    scratch += [
        pltpu.VMEM((C, TEMB), BF16),
        pltpu.VMEM((TEMB, TEMB), BF16),
        pltpu.VMEM((C, TEMB), BF16),
        pltpu.VMEM((3, DEPTH, C), BF16),
        pltpu.VMEM((3, DEPTH, C), BF16),
        pltpu.VMEM((DEPTH, 3 * REST), BF16),
        pltpu.VMEM((DEPTH, 3 * REST), BF16),
        pltpu.VMEM((128, C), BF16),
        pltpu.VMEM((2, WIN, MAIN), F32),
        pltpu.VMEM((2, 2, WIN, C), F32),
        pltpu.VMEM((2, 3, STRIDE, C), F32),
        pltpu.VMEM((3, 8, C), F32),
        pltpu.VMEM((C, C), BF16),
        pltpu.VMEM((8, C), F32),
        pltpu.VMEM((2, WIN + 2, WIN, 128), F32),
        pltpu.VMEM((2, WIN, WIN, C), BF16),
        pltpu.VMEM((2, WIN + 2, WIN, 4 * MAIN), BF16),
        pltpu.VMEM((2, WIN, WIN, C), F32),
        pltpu.VMEM((3, STRIDE, C), F32),
        pltpu.VMEM((WIN // 2 + 1, 2 * STRIDE, 4 * MAIN), BF16),
        pltpu.VMEM((WIN // 2, 2 * STRIDE, 4 * MAIN), BF16),
        pltpu.VMEM((band_rows, STRIDE, C), F32),
        pltpu.VMEM((2, 8, C), F32),
        pltpu.VMEM((2, 8, C), F32),
        pltpu.VMEM((2, 2, 8, C), F32),
        pltpu.VMEM((2, 2, 8, C), F32),
        pltpu.VMEM((n_prev // 2, 2 * STRIDE, C), BF16),
        pltpu.VMEM((n_next // 2, 2 * STRIDE, C), BF16),
        pltpu.VMEM((n_next // 2, 2 * STRIDE, C), BF16),
        pltpu.VMEM((n_prev // 2, 2 * STRIDE, C), BF16),
        pltpu.SemaphoreType.DMA((4,)),
        pltpu.SemaphoreType.DMA((10,)),
        pltpu.SemaphoreType.DMA((3,)),
        pltpu.SemaphoreType.DMA((2, 18)),
        pltpu.SemaphoreType.DMA((5,)),
        pltpu.SemaphoreType.DMA((5,)),
        pltpu.SemaphoreType.DMA((2,)),
        pltpu.SemaphoreType.DMA((2,)),
    ]
    return pl.pallas_call(
        functools.partial(body, plan, row_axis),
        out_shape=jax.ShapeDtypeStruct((STRIDE, STRIDE, C), F32),
        in_specs=[hbm] * 19,
        out_specs=vmem,
        scratch_shapes=scratch,
        compiler_params=pltpu.CompilerParams(
            collective_id=ident, has_side_effects=True, vmem_limit_bytes=56 * 1024 * 1024
        ),
        cost_estimate=pl.CostEstimate(
            flops=3 * 2 * 1024 * 2880 * 320, bytes_accessed=10**7, transcendentals=10**6
        ),
        name="panorama_block",
    )(*operands)


def on_device(
    row_axis,
    latent,
    offsets,
    timestep,
    conv_in_weight,
    conv_in_bias,
    norm_one_gain,
    norm_one_shift,
    conv_one_weight,
    conv_one_bias,
    time_one_weight,
    time_one_bias,
    time_two_weight,
    time_two_bias,
    time_proj_weight,
    time_proj_bias,
    norm_two_gain,
    norm_two_shift,
    conv_two_weight,
    conv_two_bias,
):
    operands = (
        offsets,
        timestep,
        latent,
        conv_in_weight,
        conv_in_bias,
        norm_one_gain,
        norm_one_shift,
        conv_one_bias,
        time_proj_bias,
        norm_two_gain,
        norm_two_shift,
        conv_two_bias,
        time_one_bias,
        time_two_bias,
        conv_one_weight,
        conv_two_weight,
        time_one_weight,
        time_two_weight,
        time_proj_weight.T,
    )
    branches = [
        functools.partial(block_kernel, name, row_axis, place)
        for place, name in enumerate(("high", "mid", "low"))
    ]
    return lax.switch(2 - (offsets[0] >> 3), branches, operands)


def solution(mesh):
    return jax.shard_map(
        functools.partial(on_device, mesh.shape["rows"]),
        mesh=mesh,
        in_specs=(P(None, "rows", "cols"),) + (P(),) * 18,
        out_specs=P("rows", "cols", None),
        check_vma=False,
    )
```

```python
import functools
import math

import jax
import jax.numpy as jnp
from jax import lax
from jax.experimental import pallas as pl
from jax.experimental.pallas import tpu as pltpu
from jax.sharding import PartitionSpec as P

C = 320
TEMB = 1280
LATC = 4
GROUPS = 32
STRIDE = 24
WIN = 32
HALF = C // 2
SIZE = C // GROUPS
MAIN = 256
REST = C - MAIN
DEPTH = 3 * C
CHUNKS = 4
ROWS = WIN // CHUNKS
EPS = 1e-05
AREA = WIN * WIN
MESH = pl.DeviceIdType.MESH
F32 = jnp.float32
BF16 = jnp.bfloat16

PLANS = {
    "top": dict(
        low=20, high=23, lead=1, prev=4, next=8, first=[(12, 4, 2, 4), (0, 2, 0, 1)], then=[(2, 10, 1, 2)]
    ),
    "mid": dict(
        low=8, high=19, lead=1, prev=16, next=4, first=[(0, 8, 0, 3), (14, 2, 3, 4)], then=[(8, 6, 0, 0)]
    ),
    "low": dict(low=0, high=7, lead=0, prev=0, next=16, first=[(8, 8, 1, 4)], then=[(0, 8, 0, 1)]),
}
FRONT = 12
BACK = 12


def silu(value):
    half = 0.5 * value
    return half * jnp.tanh(half) + half


def iota(shape, dim):
    return lax.broadcasted_iota(jnp.int32, shape, dim)


def split3(value):
    top = value.astype(BF16).astype(F32)
    left = value - top
    mid = left.astype(BF16).astype(F32)
    return jnp.concatenate([top, mid, left - mid, jnp.zeros_like(value)], axis=0).astype(BF16)


def group_sum(value, groups):
    parts = jnp.dot(split3(value), groups, preferred_element_type=F32)
    return parts[0:8] + parts[8:16] + parts[16:24]


def body(
    plan,
    row_axis,
    offsets_hbm,
    timestep_hbm,
    latent_hbm,
    conv_in_hbm,
    conv_in_bias_hbm,
    gain_one_hbm,
    move_one_hbm,
    conv_one_bias_hbm,
    proj_bias_hbm,
    gain_two_hbm,
    move_two_hbm,
    conv_two_bias_hbm,
    time_one_bias_hbm,
    time_two_bias_hbm,
    conv_one_hbm,
    conv_two_hbm,
    time_one_hbm,
    time_two_hbm,
    time_proj_hbm,
    out_ref,
    offsets_ref,
    timestep_ref,
    latent_ref,
    conv_in_ref,
    ext,
    conv_in_bias,
    gain_one,
    move_one,
    conv_one_bias,
    proj_bias,
    gain_two,
    move_two,
    conv_two_bias,
    time_one_bias,
    time_two_bias,
    time_one,
    time_two,
    time_proj,
    w_one,
    w_two,
    tail_one,
    tail_two,
    w_in,
    onehot,
    edge,
    cover,
    wrap,
    groups,
    shift_vec,
    lat,
    start,
    act,
    inner,
    last,
    tops,
    even,
    odd,
    band,
    means,
    spreads,
    norm_one,
    norm_two,
    send_prev,
    send_next,
    from_prev,
    from_next,
    in_sems,
    vec_sems,
    time_sems,
    w_sems,
    lat_send,
    lat_recv,
    out_send,
    out_recv,
):
    lead, n_prev, n_next, front = plan["lead"], plan["prev"], plan["next"], FRONT
    row, col = lax.axis_index("rows"), lax.axis_index("cols")
    after, before = lax.rem(row + 1, row_axis), lax.rem(row + row_axis - 1, row_axis)
    other = 1 - col
    barrier = pltpu.get_barrier_semaphore()
    friends = [(before, col), (before, other), (row, other), (after, col), (after, other)]
    for friend in friends:
        pl.semaphore_signal(barrier, inc=1, device_id=friend, device_id_type=MESH)

    arguments = [
        pltpu.make_async_copy(latent_hbm, latent_ref, in_sems.at[0]),
        pltpu.make_async_copy(offsets_hbm, offsets_ref, in_sems.at[1]),
        pltpu.make_async_copy(timestep_hbm, timestep_ref, in_sems.at[2]),
        pltpu.make_async_copy(conv_in_hbm, conv_in_ref, in_sems.at[3]),
    ]
    for copy in arguments:
        copy.start()
    small = [
        pltpu.make_async_copy(time_one_hbm, time_one, time_sems.at[0]),
        pltpu.make_async_copy(time_two_hbm, time_two, time_sems.at[1]),
        pltpu.make_async_copy(time_proj_hbm, time_proj, time_sems.at[2]),
    ]
    vectors = [
        (conv_in_bias_hbm, conv_in_bias),
        (gain_one_hbm, gain_one),
        (move_one_hbm, move_one),
        (conv_one_bias_hbm, conv_one_bias),
        (proj_bias_hbm, proj_bias),
        (gain_two_hbm, gain_two),
        (move_two_hbm, move_two),
        (conv_two_bias_hbm, conv_two_bias),
        (time_one_bias_hbm, time_one_bias),
        (time_two_bias_hbm, time_two_bias),
    ]
    for place, (source, target) in enumerate(vectors):
        small.append(pltpu.make_async_copy(source, target, vec_sems.at[place]))
    for copy in small:
        copy.start()

    def line_of(ref):
        return ref[...].reshape(1, ref.shape[0])

    def weight_copies(source, target, slot):
        copies = []
        for dy in range(3):
            for dx in range(3):
                copies.append(
                    pltpu.make_async_copy(
                        source.at[dy, dx, pl.ds(0, MAIN)],
                        target.at[dy, pl.ds(dx * MAIN, MAIN)],
                        w_sems.at[slot, dy * 6 + dx * 2],
                    )
                )
                copies.append(
                    pltpu.make_async_copy(
                        source.at[dy, dx, pl.ds(MAIN, REST)],
                        target.at[dy, pl.ds(3 * MAIN + dx * REST, REST)],
                        w_sems.at[slot, dy * 6 + dx * 2 + 1],
                    )
                )
        return copies

    copies_one = weight_copies(conv_one_hbm, w_one, 0)
    copies_two = weight_copies(conv_two_hbm, w_two, 1)

    for copy in arguments:
        copy.wait()
    row_off = jnp.clip(offsets_ref[0], plan["low"], plan["high"])
    col_off = offsets_ref[1]

    own_at = 24 * lead
    blank = jnp.zeros((STRIDE, 8), F32)
    pieces = []
    for channel in range(LATC):
        pieces += [latent_ref[channel].astype(F32), blank]
    ext[0, own_at : own_at + STRIDE, :] = jnp.concatenate(pieces, axis=1)

    pl.semaphore_wait(barrier, len(friends))

    own = ext.at[0, pl.ds(own_at, STRIDE)]
    heads = 8 if lead else 16
    head = ext.at[0, pl.ds(own_at, heads)]
    moves = [
        (own, ext.at[1, pl.ds(own_at, STRIDE)], (row, other)),
        (head, ext.at[0, pl.ds(own_at + STRIDE, heads)], (before, col)),
        (head, ext.at[1, pl.ds(own_at + STRIDE, heads)], (before, other)),
    ]
    if lead:
        moves += [
            (own, ext.at[0, pl.ds(0, STRIDE)], (after, col)),
            (own, ext.at[1, pl.ds(0, STRIDE)], (after, other)),
        ]
    lat_copies = []
    for place, (source, target, device) in enumerate(moves):
        copy = pltpu.make_async_remote_copy(
            src_ref=source,
            dst_ref=target,
            send_sem=lat_send.at[place],
            recv_sem=lat_recv.at[place],
            device_id=device,
            device_id_type=MESH,
        )
        copy.start()
        lat_copies.append(copy)

    tap = iota((MAIN, 128), 1)
    from_lane = iota((MAIN, 128), 0)
    same = ((from_lane & 127) >> 5) == (tap & 3)
    pick = jnp.where(same & (tap < 9 * LATC), 1.0, 0.0).astype(BF16)
    first_g, second_g = iota((C, C), 0), iota((C, C), 1)
    low_g = second_g - lax.rem(second_g, SIZE)
    groups[...] = jnp.where((first_g >= low_g) & (first_g < low_g + SIZE), 1.0, 0.0).astype(BF16)
    w_in[...] = jnp.zeros_like(w_in)
    w_in[0 : 9 * LATC, :] = jnp.concatenate(
        [conv_in_ref[dy, dx].astype(F32) for dy in range(3) for dx in range(3)], axis=0
    ).astype(BF16)

    slot = iota((WIN, C), 0)
    slot_wide = iota((WIN, MAIN), 0)
    lane_wide = iota((WIN, MAIN), 1)
    lane_col = lane_wide & 31
    lane_at = jnp.where(lane_col < STRIDE, (lane_wide >> 7) * STRIDE + lane_col, -100)
    for window in range(2):
        begin = col_off - 24 * window
        place = (slot_wide - begin) & 31
        column = begin + place
        column = jnp.where(column < 0, column + 48, column)
        column = jnp.where(column >= 48, column - 48, column)
        onehot[window] = jnp.where(lane_at == column, 1.0, 0.0)
        place = (slot - begin) & 31
        edge[window, 0] = jnp.where(place > 0, 1.0, 0.0)
        edge[window, 1] = jnp.where(place < WIN - 1, 1.0, 0.0)
    mine = iota((STRIDE, C), 0)
    near = iota((8, C), 0)
    for tap in range(3):
        for window in range(2):
            covered = (mine >= col_off) if window == 0 else (mine <= col_off + 7)
            mask = jnp.where(covered, 1.0, 0.0)
            if tap != 1:
                mask = mask * edge[window, tap // 2, 0:STRIDE]
            cover[window, tap] = mask
        mask = jnp.where(near <= col_off - 17, 1.0, 0.0)
        if tap != 1:
            mask = mask * edge[0, tap // 2, 16:24]
        wrap[tap] = mask
    for window in range(2):
        lat[window, 0] = jnp.zeros((WIN, 128), F32)
        lat[window, WIN + 1] = jnp.zeros((WIN, 128), F32)
        act[window, 0] = jnp.zeros((WIN, 4 * MAIN), BF16)
        act[window, WIN + 1] = jnp.zeros((WIN, 4 * MAIN), BF16)
    last[...] = jnp.zeros_like(last)
    band[0:front] = jnp.zeros((front, STRIDE, C), F32)
    band[front + WIN :] = jnp.zeros((BACK, STRIDE, C), F32)

    for copy in small:
        copy.wait()
    for copy in copies_one:
        copy.start()
    freq = jnp.exp(-math.log(10000.0) * iota((8, HALF), 1).astype(F32) / HALF)
    angle = timestep_ref[0].astype(F32) * freq
    cosine = jnp.concatenate([jnp.cos(angle)] * 2, axis=0).astype(BF16)
    sine = jnp.concatenate([jnp.sin(angle)] * 2, axis=0).astype(BF16)
    hidden = jnp.dot(cosine, time_one[0:HALF, :], preferred_element_type=F32)
    hidden += jnp.dot(sine, time_one[HALF:C, :], preferred_element_type=F32)
    hidden = silu(hidden + line_of(time_one_bias)).astype(BF16)
    hidden = jnp.dot(hidden, time_two[...], preferred_element_type=F32)
    hidden = silu(hidden + line_of(time_two_bias)).astype(BF16)
    shift = lax.dot_general(
        hidden, time_proj[...], (((1,), (1,)), ((), ())), preferred_element_type=F32
    )
    shift_vec[...] = shift[0:8] + line_of(proj_bias) + line_of(conv_one_bias)

    for copy in lat_copies:
        copy.wait_recv()
    for copy in copies_two:
        copy.start()

    lane = iota((1, WIN, 128), 2) >> 2
    lane_row = lane // 3
    lane_col = lane - 3 * lane_row

    def fold(value):
        return jnp.sum(value.reshape(-1, 8, C), axis=0)

    def keep_moments(window, value):
        pivot = value[0:1]
        once = jnp.zeros((8, C), F32)
        twice = jnp.zeros((8, C), F32)
        for at in range(0, AREA, 256):
            diff = value[at : at + 256] - pivot
            once = once + fold(diff)
            twice = twice + fold(diff * diff)
        once = jnp.sum(once, axis=0, keepdims=True) * (1.0 / AREA)
        twice = jnp.sum(twice, axis=0, keepdims=True) * (1.0 / AREA)
        means[window] = jnp.broadcast_to(pivot + once, (8, C))
        spreads[window] = jnp.broadcast_to(jnp.maximum(twice - once * once, 0.0), (8, C))

    def norm_lines(target, gain, offset):
        spare = jnp.zeros((6, C), F32)
        mean = jnp.concatenate([means[0, 0:1], means[1, 0:1], spare], axis=0)
        spread = jnp.concatenate([spreads[0, 0:1], spreads[1, 0:1], spare], axis=0)
        centre = group_sum(mean, groups[...]) * (1.0 / SIZE)
        diff = mean - centre
        var = group_sum(spread + diff * diff, groups[...]) * (1.0 / SIZE)
        scale = 0.5 * gain / jnp.sqrt(var + EPS)
        move = 0.5 * offset - centre * scale
        for window in range(2):
            target[window, 0] = jnp.broadcast_to(scale[window : window + 1], (8, C))
            target[window, 1] = jnp.broadcast_to(move[window : window + 1], (8, C))

    def run_in(window, _):
        chosen = onehot[window]
        lines = []
        for line in range(WIN):
            at = row_off + line
            left = ext[0, pl.ds(at, 1), :]
            right = ext[1, pl.ds(at, 1), :]
            lines.append((jnp.concatenate([left, right], axis=1) * chosen).astype(BF16))
        got = jnp.dot(jnp.concatenate(lines, axis=0), pick, preferred_element_type=F32)
        lat[window, 1 : WIN + 1] = got.reshape(WIN, WIN, 128)
        full = lat[window]
        less = pltpu.roll(full, 1, 1) * edge[window, 0, :, 0:128]
        more = pltpu.roll(full, WIN - 1, 1) * edge[window, 1, :, 0:128]
        wide = jnp.where(lane_col == 0, less, jnp.where(lane_col == 1, full, more))
        patch = jnp.where(
            lane_row == 0,
            wide[0:WIN],
            jnp.where(lane_row == 1, wide[1 : WIN + 1], wide[2 : WIN + 2]),
        )
        patch = patch.reshape(AREA, 128).astype(BF16)
        value = jnp.dot(patch, w_in[...], preferred_element_type=F32) + line_of(conv_in_bias)
        value = value.astype(BF16)
        start[window] = value.reshape(WIN, WIN, C)
        keep_moments(window, value.astype(F32))
        return 0

    lax.fori_loop(0, 2, run_in, 0)
    norm_lines(norm_one, line_of(gain_one), line_of(move_one))

    def three_columns(value, window):
        less = pltpu.roll(value, 1, 1) * edge[window, 0]
        more = pltpu.roll(value, WIN - 1, 1) * edge[window, 1]
        return less, value, more

    def rests(parts):
        return jnp.concatenate([part[..., MAIN:C] for part in parts], axis=-1).astype(BF16)

    def store_act(window, chunk, parts):
        at = pl.ds(1 + chunk * ROWS, ROWS)
        for place, part in enumerate(parts):
            act[window, at, :, place * MAIN : (place + 1) * MAIN] = part[:, :, 0:MAIN].astype(BF16)
        act[window, at, :, 3 * MAIN : DEPTH] = rests(parts)

    def activate(value, lines, window):
        half = value * lines[window, 0, 0:1] + lines[window, 1, 0:1]
        return half * jnp.tanh(half) + half

    def run_act(step, _):
        window, chunk = step // CHUNKS, step % CHUNKS
        value = start[window, pl.ds(chunk * ROWS, ROWS)].astype(F32)
        value = activate(value, norm_one, window)
        store_act(window, chunk, three_columns(value, window))
        return 0

    lax.fori_loop(0, CHUNKS, run_act, 0)

    def tails(weights, target):
        blocks = [weights[dy, :, MAIN:C] for dy in range(3)]
        target[...] = jnp.concatenate(blocks, axis=1)

    def taps(sources, whole, width, weights, tail):
        pixels = sources[0].shape[0]
        total = jnp.dot(sources[0], weights[0, :, 0:MAIN], preferred_element_type=F32)
        total += jnp.dot(sources[1], weights[1, :, 0:MAIN], preferred_element_type=F32)
        total += jnp.dot(sources[2], weights[2, :, 0:MAIN], preferred_element_type=F32)
        rest = jnp.dot(whole, tail[...], preferred_element_type=F32)
        left = (
            rest[0:pixels, 0:REST]
            + rest[width : width + pixels, REST : 2 * REST]
            + rest[2 * width : 2 * width + pixels, 2 * REST : 3 * REST]
        )
        return jnp.concatenate([total, left], axis=1)

    for copy in copies_one:
        copy.wait()
    tails(w_one, tail_one)

    def run_one(window, _):
        sources = [act[window, dy : dy + WIN, :, 0:DEPTH].reshape(AREA, DEPTH) for dy in range(3)]
        whole = act[window, :, :, 0:DEPTH].reshape((WIN + 2) * WIN, DEPTH)
        value = taps(sources, whole, WIN, w_one, tail_one) + shift_vec[0:1, :]
        inner[window] = value.reshape(WIN, WIN, C)
        keep_moments(window, value)
        return 0

    for step in range(CHUNKS, 2 * CHUNKS):
        run_act(step, 0)
    run_one(0, 0)
    run_one(1, 0)
    norm_lines(norm_two, line_of(gain_two), line_of(move_two))

    def merge(first, second, tap):
        main = first[:, 0:STRIDE] * cover[0, tap] + second[:, 0:STRIDE] * cover[1, tap]
        extra = first[:, 16:24] * wrap[tap]
        return jnp.concatenate([main[:, 0:8] + extra, main[:, 8:STRIDE]], axis=1)

    def store_pairs(target, at, count, parts):
        parts = [part.reshape(count, 2 * STRIDE, C) for part in parts]
        for place, part in enumerate(parts):
            target[at, :, place * MAIN : (place + 1) * MAIN] = part[:, :, 0:MAIN].astype(BF16)
        target[at, :, 3 * MAIN : DEPTH] = rests(parts)

    def run_merge(chunk, _):
        lines = []
        for window in range(2):
            value = inner[window, pl.ds(chunk * ROWS, ROWS)]
            value = activate(value, norm_two, window).astype(BF16).astype(F32)
            lines.append((pltpu.roll(value, 1, 1), value, pltpu.roll(value, WIN - 1, 1)))
        parts = [merge(lines[0][tap], lines[1][tap], tap) for tap in range(3)]
        at = pl.ds(chunk * (ROWS // 2), ROWS // 2)
        store_pairs(odd, at, ROWS // 2, parts)
        late = []
        for tap in range(3):
            late.append(jnp.concatenate([last[tap][None], parts[tap][0 : ROWS - 1]], axis=0))
            last[tap] = parts[tap][ROWS - 1]
            tops[chunk, tap] = parts[tap][0]
        store_pairs(even, at, ROWS // 2, late)
        return 0

    def merge_chunks(begin, end):
        if begin == 0:
            last[...] = jnp.zeros_like(last)
        lax.fori_loop(begin, end, run_merge, 0)
        if end == CHUNKS:
            lower = [jnp.zeros((1, STRIDE, C), F32)] * 3
        elif end in merged:
            lower = [tops[end, tap][None] for tap in range(3)]
        else:
            lower = None
        if lower is not None:
            ends = [jnp.concatenate([last[tap][None], lower[tap]], axis=0) for tap in range(3)]
            store_pairs(even, pl.ds(end * (ROWS // 2), 1), 1, ends)
        merged.update(range(begin, end))

    merged = set()

    for copy in copies_two:
        copy.wait()
    tails(w_two, tail_two)
    counted = cover[0, 1] + cover[1, 1]
    counted = jnp.concatenate([counted[0:8] + wrap[1], counted[8:STRIDE]], axis=0)

    def run_two(pair, count):
        def flat(source, at, number):
            return source[at : at + number, :, 0:DEPTH].reshape(number * 2 * STRIDE, DEPTH)

        sources = [flat(even, pair, count), flat(odd, pair, count), flat(even, pair + 1, count)]
        value = taps(sources, flat(even, pair, count + 1), STRIDE, w_two, tail_two)
        value = value.reshape(2 * count, STRIDE, C)
        at = slice(2 * pair, 2 * pair + 2 * count)
        first, second = start[0, at].astype(F32), start[1, at].astype(F32)
        value = value + merge(first, second, 1) + counted * line_of(conv_two_bias)
        band[front + 2 * pair : front + 2 * pair + 2 * count] = value

    def stage(target, base, count):
        def one(pair, _):
            upper = band[base + 2 * pair]
            lower = band[base + 2 * pair + 1]
            target[pair] = jnp.concatenate([upper, lower], axis=0).astype(BF16)
            return 0

        lax.fori_loop(0, count // 2, one, 0)

    started = []

    def send(source, target, device, place):
        copy = pltpu.make_async_remote_copy(
            src_ref=source,
            dst_ref=target,
            send_sem=out_send.at[place],
            recv_sem=out_recv.at[place],
            device_id=device,
            device_id_type=MESH,
        )
        copy.start()
        started.append(copy)

    for pair, count, begin, end in plan["first"]:
        if end > begin:
            merge_chunks(begin, end)
        run_two(pair, count)
        if pair == 0:
            stage(send_prev, FRONT + 24 * lead - row_off - n_prev, n_prev)
            send(send_prev, from_next, (before, col), 0)
        else:
            stage(send_next, FRONT + 24 + 24 * lead - row_off, n_next)
            send(send_next, from_prev, (after, col), 1)

    for pair, count, begin, end in plan["then"]:
        if end > begin:
            merge_chunks(begin, end)
        run_two(pair, count)
    for copy in started:
        copy.wait_recv()

    scale_cols = 1.0 / counted

    def finish(pair, has_prev, has_next):
        pieces = []
        for line in range(2):
            at = 2 * pair + line
            pieces.append(band[front + 24 * lead - row_off + at])
        value = jnp.concatenate(pieces, axis=0)
        if has_prev:
            value = value + from_prev[pair].astype(F32)
        if has_next:
            value = value + from_next[pair - (STRIDE - n_prev) // 2].astype(F32)
        for line in range(2):
            at = 2 * pair + line
            twice = lax.rem(at - row_off + 24, 24) < 8
            scale = jnp.where(twice, 0.5, 1.0)
            out_ref[at] = value[line * STRIDE : (line + 1) * STRIDE] * (scale_cols * scale)

    marks = sorted({0, n_next // 2, (STRIDE - n_prev) // 2, STRIDE // 2})
    for low, high in zip(marks[:-1], marks[1:]):
        has_prev = low < n_next // 2
        has_next = low >= (STRIDE - n_prev) // 2

        def one(pair, _, has_prev=has_prev, has_next=has_next):
            finish(pair, has_prev, has_next)
            return 0

        lax.fori_loop(low, high, one, 0)

    for copy in lat_copies + started:
        copy.wait_send()


def block_kernel(name, row_axis, ident, operands):
    plan = PLANS[name]
    hbm = pl.BlockSpec(memory_space=pl.ANY)
    vmem = pl.BlockSpec(memory_space=pltpu.VMEM)
    n_prev, n_next = max(plan["prev"], 2), max(plan["next"], 2)
    ext_rows = 56 if plan["lead"] else 40
    band_rows = FRONT + WIN + BACK
    scratch = [
        pltpu.SMEM((2,), jnp.int32),
        pltpu.SMEM((1,), jnp.int32),
        pltpu.VMEM((LATC, STRIDE, STRIDE), BF16),
        pltpu.VMEM((3, 3, LATC, C), BF16),
        pltpu.VMEM((2, ext_rows, 128), F32),
    ]
    scratch += [pltpu.VMEM((C,), F32)] * 8 + [pltpu.VMEM((TEMB,), F32)] * 2
    scratch += [
        pltpu.VMEM((C, TEMB), BF16),
        pltpu.VMEM((TEMB, TEMB), BF16),
        pltpu.VMEM((C, TEMB), BF16),
        pltpu.VMEM((3, DEPTH, C), BF16),
        pltpu.VMEM((3, DEPTH, C), BF16),
        pltpu.VMEM((DEPTH, 3 * REST), BF16),
        pltpu.VMEM((DEPTH, 3 * REST), BF16),
        pltpu.VMEM((128, C), BF16),
        pltpu.VMEM((2, WIN, MAIN), F32),
        pltpu.VMEM((2, 2, WIN, C), F32),
        pltpu.VMEM((2, 3, STRIDE, C), F32),
        pltpu.VMEM((3, 8, C), F32),
        pltpu.VMEM((C, C), BF16),
        pltpu.VMEM((8, C), F32),
        pltpu.VMEM((2, WIN + 2, WIN, 128), F32),
        pltpu.VMEM((2, WIN, WIN, C), BF16),
        pltpu.VMEM((2, WIN + 2, WIN, 4 * MAIN), BF16),
        pltpu.VMEM((2, WIN, WIN, C), F32),
        pltpu.VMEM((3, STRIDE, C), F32),
        pltpu.VMEM((CHUNKS, 3, STRIDE, C), F32),
        pltpu.VMEM((WIN // 2 + 1, 2 * STRIDE, 4 * MAIN), BF16),
        pltpu.VMEM((WIN // 2, 2 * STRIDE, 4 * MAIN), BF16),
        pltpu.VMEM((band_rows, STRIDE, C), F32),
        pltpu.VMEM((2, 8, C), F32),
        pltpu.VMEM((2, 8, C), F32),
        pltpu.VMEM((2, 2, 8, C), F32),
        pltpu.VMEM((2, 2, 8, C), F32),
        pltpu.VMEM((n_prev // 2, 2 * STRIDE, C), BF16),
        pltpu.VMEM((n_next // 2, 2 * STRIDE, C), BF16),
        pltpu.VMEM((n_next // 2, 2 * STRIDE, C), BF16),
        pltpu.VMEM((n_prev // 2, 2 * STRIDE, C), BF16),
        pltpu.SemaphoreType.DMA((4,)),
        pltpu.SemaphoreType.DMA((10,)),
        pltpu.SemaphoreType.DMA((3,)),
        pltpu.SemaphoreType.DMA((2, 18)),
        pltpu.SemaphoreType.DMA((5,)),
        pltpu.SemaphoreType.DMA((5,)),
        pltpu.SemaphoreType.DMA((2,)),
        pltpu.SemaphoreType.DMA((2,)),
    ]
    return pl.pallas_call(
        functools.partial(body, plan, row_axis),
        out_shape=jax.ShapeDtypeStruct((STRIDE, STRIDE, C), F32),
        in_specs=[hbm] * 19,
        out_specs=vmem,
        scratch_shapes=scratch,
        compiler_params=pltpu.CompilerParams(
            collective_id=ident, has_side_effects=True, vmem_limit_bytes=56 * 1024 * 1024
        ),
        cost_estimate=pl.CostEstimate(
            flops=3 * 2 * 1024 * 2880 * 320, bytes_accessed=10**7, transcendentals=10**6
        ),
        name="panorama_block",
    )(*operands)


def on_device(
    row_axis,
    latent,
    offsets,
    timestep,
    conv_in_weight,
    conv_in_bias,
    norm_one_gain,
    norm_one_shift,
    conv_one_weight,
    conv_one_bias,
    time_one_weight,
    time_one_bias,
    time_two_weight,
    time_two_bias,
    time_proj_weight,
    time_proj_bias,
    norm_two_gain,
    norm_two_shift,
    conv_two_weight,
    conv_two_bias,
):
    operands = (
        offsets,
        timestep,
        latent,
        conv_in_weight,
        conv_in_bias,
        norm_one_gain,
        norm_one_shift,
        conv_one_bias,
        time_proj_bias,
        norm_two_gain,
        norm_two_shift,
        conv_two_bias,
        time_one_bias,
        time_two_bias,
        conv_one_weight,
        conv_two_weight,
        time_one_weight,
        time_two_weight,
        time_proj_weight.T,
    )
    branches = [
        functools.partial(block_kernel, name, row_axis, place)
        for place, name in enumerate(("top", "mid", "low"))
    ]
    return lax.switch(2 - (((offsets[0] + 4) * 11) >> 7), branches, operands)


def solution(mesh):
    return jax.shard_map(
        functools.partial(on_device, mesh.shape["rows"]),
        mesh=mesh,
        in_specs=(P(None, "rows", "cols"),) + (P(),) * 18,
        out_specs=P("rows", "cols", None),
        check_vma=False,
    )
```

```python
import functools
import math

import jax
import jax.numpy as jnp
from jax import lax
from jax.experimental import pallas as pl
from jax.experimental.pallas import tpu as pltpu
from jax.sharding import PartitionSpec as P

C = 320
TEMB = 1280
LATC = 4
GROUPS = 32
STRIDE = 24
WIN = 32
HALF = C // 2
SIZE = C // GROUPS
MAIN = 256
REST = C - MAIN
DEPTH = 3 * C
CHUNKS = 4
ROWS = WIN // CHUNKS
EPS = 1e-05
AREA = WIN * WIN
MESH = pl.DeviceIdType.MESH
F32 = jnp.float32
BF16 = jnp.bfloat16

PLANS = {
    "top": dict(
        low=20,
        high=23,
        lead=1,
        prev=4,
        next=8,
        first=[(12, 4, 2, 4, "next", 0, 4), (0, 2, 0, 1, "prev", 0, 2)],
        then=[(2, 10, 1, 2)],
    ),
    "mid": dict(
        low=8,
        high=19,
        lead=1,
        prev=16,
        next=4,
        first=[
            (0, 4, 0, 2, "prev", 0, 4),
            (4, 4, 2, 3, "prev", 4, 8),
            (14, 2, 3, 4, "next", 0, 2),
        ],
        then=[(8, 6, 0, 0)],
    ),
    "low": dict(
        low=0,
        high=7,
        lead=0,
        prev=0,
        next=16,
        first=[(12, 4, 2, 4, "next", 4, 8), (8, 4, 1, 2, "next", 0, 4)],
        then=[(0, 8, 0, 1)],
    ),
}
FRONT = 12
BACK = 12


def silu(value):
    half = 0.5 * value
    return half * jnp.tanh(half) + half


def iota(shape, dim):
    return lax.broadcasted_iota(jnp.int32, shape, dim)


def split3(value):
    top = value.astype(BF16).astype(F32)
    left = value - top
    mid = left.astype(BF16).astype(F32)
    return jnp.concatenate([top, mid, left - mid, jnp.zeros_like(value)], axis=0).astype(BF16)


def group_sum(value, groups):
    parts = jnp.dot(split3(value), groups, preferred_element_type=F32)
    return parts[0:8] + parts[8:16] + parts[16:24]


def body(
    plan,
    row_axis,
    offsets_hbm,
    timestep_hbm,
    latent_hbm,
    conv_in_hbm,
    conv_in_bias_hbm,
    gain_one_hbm,
    move_one_hbm,
    conv_one_bias_hbm,
    proj_bias_hbm,
    gain_two_hbm,
    move_two_hbm,
    conv_two_bias_hbm,
    time_one_bias_hbm,
    time_two_bias_hbm,
    conv_one_hbm,
    conv_two_hbm,
    time_one_hbm,
    time_two_hbm,
    time_proj_hbm,
    out_ref,
    offsets_ref,
    timestep_ref,
    latent_ref,
    conv_in_ref,
    ext,
    conv_in_bias,
    gain_one,
    move_one,
    conv_one_bias,
    proj_bias,
    gain_two,
    move_two,
    conv_two_bias,
    time_one_bias,
    time_two_bias,
    time_one,
    time_two,
    time_proj,
    w_one,
    w_two,
    tail_one,
    tail_two,
    w_in,
    onehot,
    edge,
    cover,
    wrap,
    groups,
    shift_vec,
    lat,
    start,
    act,
    inner,
    last,
    tops,
    even,
    odd,
    band,
    means,
    spreads,
    norm_one,
    norm_two,
    send_prev,
    send_next,
    from_prev,
    from_next,
    in_sems,
    vec_sems,
    time_sems,
    w_sems,
    lat_send,
    lat_recv,
    out_send,
    out_recv,
):
    lead, n_prev, n_next, front = plan["lead"], plan["prev"], plan["next"], FRONT
    row, col = lax.axis_index("rows"), lax.axis_index("cols")
    after, before = lax.rem(row + 1, row_axis), lax.rem(row + row_axis - 1, row_axis)
    other = 1 - col
    barrier = pltpu.get_barrier_semaphore()
    friends = [(before, col), (before, other), (row, other), (after, col), (after, other)]
    for friend in friends:
        pl.semaphore_signal(barrier, inc=1, device_id=friend, device_id_type=MESH)

    arguments = [
        pltpu.make_async_copy(latent_hbm, latent_ref, in_sems.at[0]),
        pltpu.make_async_copy(offsets_hbm, offsets_ref, in_sems.at[1]),
        pltpu.make_async_copy(timestep_hbm, timestep_ref, in_sems.at[2]),
        pltpu.make_async_copy(conv_in_hbm, conv_in_ref, in_sems.at[3]),
    ]
    for copy in arguments:
        copy.start()
    small = [
        pltpu.make_async_copy(time_one_hbm, time_one, time_sems.at[0]),
        pltpu.make_async_copy(time_two_hbm, time_two, time_sems.at[1]),
        pltpu.make_async_copy(time_proj_hbm, time_proj, time_sems.at[2]),
    ]
    vectors = [
        (conv_in_bias_hbm, conv_in_bias),
        (gain_one_hbm, gain_one),
        (move_one_hbm, move_one),
        (conv_one_bias_hbm, conv_one_bias),
        (proj_bias_hbm, proj_bias),
        (gain_two_hbm, gain_two),
        (move_two_hbm, move_two),
        (conv_two_bias_hbm, conv_two_bias),
        (time_one_bias_hbm, time_one_bias),
        (time_two_bias_hbm, time_two_bias),
    ]
    for place, (source, target) in enumerate(vectors):
        small.append(pltpu.make_async_copy(source, target, vec_sems.at[place]))
    for copy in small:
        copy.start()

    def line_of(ref):
        return ref[...].reshape(1, ref.shape[0])

    def weight_copies(source, target, slot):
        copies = []
        for dy in range(3):
            for dx in range(3):
                copies.append(
                    pltpu.make_async_copy(
                        source.at[dy, dx, pl.ds(0, MAIN)],
                        target.at[dy, pl.ds(dx * MAIN, MAIN)],
                        w_sems.at[slot, dy * 6 + dx * 2],
                    )
                )
                copies.append(
                    pltpu.make_async_copy(
                        source.at[dy, dx, pl.ds(MAIN, REST)],
                        target.at[dy, pl.ds(3 * MAIN + dx * REST, REST)],
                        w_sems.at[slot, dy * 6 + dx * 2 + 1],
                    )
                )
        return copies

    copies_one = weight_copies(conv_one_hbm, w_one, 0)
    copies_two = weight_copies(conv_two_hbm, w_two, 1)

    for copy in arguments:
        copy.wait()
    row_off = jnp.clip(offsets_ref[0], plan["low"], plan["high"])
    col_off = offsets_ref[1]

    own_at = 24 * lead
    blank = jnp.zeros((STRIDE, 8), F32)
    pieces = []
    for channel in range(LATC):
        pieces += [latent_ref[channel].astype(F32), blank]
    ext[0, own_at : own_at + STRIDE, :] = jnp.concatenate(pieces, axis=1)

    pl.semaphore_wait(barrier, len(friends))

    own = ext.at[0, pl.ds(own_at, STRIDE)]
    heads = 8 if lead else 16
    head = ext.at[0, pl.ds(own_at, heads)]
    moves = [
        (own, ext.at[1, pl.ds(own_at, STRIDE)], (row, other)),
        (head, ext.at[0, pl.ds(own_at + STRIDE, heads)], (before, col)),
        (head, ext.at[1, pl.ds(own_at + STRIDE, heads)], (before, other)),
    ]
    if lead:
        moves += [
            (own, ext.at[0, pl.ds(0, STRIDE)], (after, col)),
            (own, ext.at[1, pl.ds(0, STRIDE)], (after, other)),
        ]
    lat_copies = []
    for place, (source, target, device) in enumerate(moves):
        copy = pltpu.make_async_remote_copy(
            src_ref=source,
            dst_ref=target,
            send_sem=lat_send.at[place],
            recv_sem=lat_recv.at[place],
            device_id=device,
            device_id_type=MESH,
        )
        copy.start()
        lat_copies.append(copy)

    tap = iota((MAIN, 128), 1)
    from_lane = iota((MAIN, 128), 0)
    same = ((from_lane & 127) >> 5) == (tap & 3)
    pick = jnp.where(same & (tap < 9 * LATC), 1.0, 0.0).astype(BF16)
    first_g, second_g = iota((C, C), 0), iota((C, C), 1)
    low_g = second_g - lax.rem(second_g, SIZE)
    groups[...] = jnp.where((first_g >= low_g) & (first_g < low_g + SIZE), 1.0, 0.0).astype(BF16)
    w_in[...] = jnp.zeros_like(w_in)
    w_in[0 : 9 * LATC, :] = jnp.concatenate(
        [conv_in_ref[dy, dx].astype(F32) for dy in range(3) for dx in range(3)], axis=0
    ).astype(BF16)

    slot = iota((WIN, C), 0)
    slot_wide = iota((WIN, MAIN), 0)
    lane_wide = iota((WIN, MAIN), 1)
    lane_col = lane_wide & 31
    lane_at = jnp.where(lane_col < STRIDE, (lane_wide >> 7) * STRIDE + lane_col, -100)
    for window in range(2):
        begin = col_off - 24 * window
        place = (slot_wide - begin) & 31
        column = begin + place
        column = jnp.where(column < 0, column + 48, column)
        column = jnp.where(column >= 48, column - 48, column)
        onehot[window] = jnp.where(lane_at == column, 1.0, 0.0)
        place = (slot - begin) & 31
        edge[window, 0] = jnp.where(place > 0, 1.0, 0.0)
        edge[window, 1] = jnp.where(place < WIN - 1, 1.0, 0.0)
    mine = iota((STRIDE, C), 0)
    near = iota((8, C), 0)
    for tap in range(3):
        for window in range(2):
            covered = (mine >= col_off) if window == 0 else (mine <= col_off + 7)
            mask = jnp.where(covered, 1.0, 0.0)
            if tap != 1:
                mask = mask * edge[window, tap // 2, 0:STRIDE]
            cover[window, tap] = mask
        mask = jnp.where(near <= col_off - 17, 1.0, 0.0)
        if tap != 1:
            mask = mask * edge[0, tap // 2, 16:24]
        wrap[tap] = mask
    for window in range(2):
        lat[window, 0] = jnp.zeros((WIN, 128), F32)
        lat[window, WIN + 1] = jnp.zeros((WIN, 128), F32)
        act[window, 0] = jnp.zeros((WIN, 4 * MAIN), BF16)
        act[window, WIN + 1] = jnp.zeros((WIN, 4 * MAIN), BF16)
    last[...] = jnp.zeros_like(last)
    band[0:front] = jnp.zeros((front, STRIDE, C), F32)
    band[front + WIN :] = jnp.zeros((BACK, STRIDE, C), F32)

    for copy in small:
        copy.wait()
    for copy in copies_one:
        copy.start()
    freq = jnp.exp(-math.log(10000.0) * iota((8, HALF), 1).astype(F32) / HALF)
    angle = timestep_ref[0].astype(F32) * freq
    cosine = jnp.concatenate([jnp.cos(angle)] * 2, axis=0).astype(BF16)
    sine = jnp.concatenate([jnp.sin(angle)] * 2, axis=0).astype(BF16)
    hidden = jnp.dot(cosine, time_one[0:HALF, :], preferred_element_type=F32)
    hidden += jnp.dot(sine, time_one[HALF:C, :], preferred_element_type=F32)
    hidden = silu(hidden + line_of(time_one_bias)).astype(BF16)
    hidden = jnp.dot(hidden, time_two[...], preferred_element_type=F32)
    hidden = silu(hidden + line_of(time_two_bias)).astype(BF16)
    shift = lax.dot_general(
        hidden, time_proj[...], (((1,), (1,)), ((), ())), preferred_element_type=F32
    )
    shift_vec[...] = shift[0:8] + line_of(proj_bias) + line_of(conv_one_bias)

    for copy in lat_copies:
        copy.wait_recv()
    for copy in copies_two:
        copy.start()

    lane = iota((1, WIN, 128), 2) >> 2
    lane_row = lane // 3
    lane_col = lane - 3 * lane_row

    def fold(value):
        return jnp.sum(value.reshape(-1, 8, C), axis=0)

    def keep_moments(window, value):
        pivot = value[0:1]
        once = jnp.zeros((8, C), F32)
        twice = jnp.zeros((8, C), F32)
        for at in range(0, AREA, 256):
            diff = value[at : at + 256] - pivot
            once = once + fold(diff)
            twice = twice + fold(diff * diff)
        once = jnp.sum(once, axis=0, keepdims=True) * (1.0 / AREA)
        twice = jnp.sum(twice, axis=0, keepdims=True) * (1.0 / AREA)
        means[window] = jnp.broadcast_to(pivot + once, (8, C))
        spreads[window] = jnp.broadcast_to(jnp.maximum(twice - once * once, 0.0), (8, C))

    def norm_lines(target, gain, offset):
        spare = jnp.zeros((6, C), F32)
        mean = jnp.concatenate([means[0, 0:1], means[1, 0:1], spare], axis=0)
        spread = jnp.concatenate([spreads[0, 0:1], spreads[1, 0:1], spare], axis=0)
        centre = group_sum(mean, groups[...]) * (1.0 / SIZE)
        diff = mean - centre
        var = group_sum(spread + diff * diff, groups[...]) * (1.0 / SIZE)
        scale = 0.5 * gain / jnp.sqrt(var + EPS)
        move = 0.5 * offset - centre * scale
        for window in range(2):
            target[window, 0] = jnp.broadcast_to(scale[window : window + 1], (8, C))
            target[window, 1] = jnp.broadcast_to(move[window : window + 1], (8, C))

    def run_in(window, _):
        chosen = onehot[window]
        lines = []
        for line in range(WIN):
            at = row_off + line
            left = ext[0, pl.ds(at, 1), :]
            right = ext[1, pl.ds(at, 1), :]
            lines.append((jnp.concatenate([left, right], axis=1) * chosen).astype(BF16))
        got = jnp.dot(jnp.concatenate(lines, axis=0), pick, preferred_element_type=F32)
        lat[window, 1 : WIN + 1] = got.reshape(WIN, WIN, 128)
        full = lat[window]
        less = pltpu.roll(full, 1, 1) * edge[window, 0, :, 0:128]
        more = pltpu.roll(full, WIN - 1, 1) * edge[window, 1, :, 0:128]
        wide = jnp.where(lane_col == 0, less, jnp.where(lane_col == 1, full, more))
        patch = jnp.where(
            lane_row == 0,
            wide[0:WIN],
            jnp.where(lane_row == 1, wide[1 : WIN + 1], wide[2 : WIN + 2]),
        )
        patch = patch.reshape(AREA, 128).astype(BF16)
        value = jnp.dot(patch, w_in[...], preferred_element_type=F32) + line_of(conv_in_bias)
        value = value.astype(BF16)
        start[window] = value.reshape(WIN, WIN, C)
        keep_moments(window, value.astype(F32))
        return 0

    lax.fori_loop(0, 2, run_in, 0)
    norm_lines(norm_one, line_of(gain_one), line_of(move_one))

    def three_columns(value, window):
        less = pltpu.roll(value, 1, 1) * edge[window, 0]
        more = pltpu.roll(value, WIN - 1, 1) * edge[window, 1]
        return less, value, more

    def rests(parts):
        return jnp.concatenate([part[..., MAIN:C] for part in parts], axis=-1).astype(BF16)

    def store_act(window, chunk, parts):
        at = pl.ds(1 + chunk * ROWS, ROWS)
        for place, part in enumerate(parts):
            act[window, at, :, place * MAIN : (place + 1) * MAIN] = part[:, :, 0:MAIN].astype(BF16)
        act[window, at, :, 3 * MAIN : DEPTH] = rests(parts)

    def activate(value, lines, window):
        half = value * lines[window, 0, 0:1] + lines[window, 1, 0:1]
        return half * jnp.tanh(half) + half

    def run_act(step, _):
        window, chunk = step // CHUNKS, step % CHUNKS
        value = start[window, pl.ds(chunk * ROWS, ROWS)].astype(F32)
        value = activate(value, norm_one, window)
        store_act(window, chunk, three_columns(value, window))
        return 0

    lax.fori_loop(0, CHUNKS, run_act, 0)

    def tails(weights, target):
        blocks = [weights[dy, :, MAIN:C] for dy in range(3)]
        target[...] = jnp.concatenate(blocks, axis=1)

    def taps(sources, whole, width, weights, tail):
        pixels = sources[0].shape[0]
        total = jnp.dot(sources[0], weights[0, :, 0:MAIN], preferred_element_type=F32)
        total += jnp.dot(sources[1], weights[1, :, 0:MAIN], preferred_element_type=F32)
        total += jnp.dot(sources[2], weights[2, :, 0:MAIN], preferred_element_type=F32)
        rest = jnp.dot(whole, tail[...], preferred_element_type=F32)
        left = (
            rest[0:pixels, 0:REST]
            + rest[width : width + pixels, REST : 2 * REST]
            + rest[2 * width : 2 * width + pixels, 2 * REST : 3 * REST]
        )
        return jnp.concatenate([total, left], axis=1)

    for copy in copies_one:
        copy.wait()
    tails(w_one, tail_one)

    def run_one(window, _):
        sources = [act[window, dy : dy + WIN, :, 0:DEPTH].reshape(AREA, DEPTH) for dy in range(3)]
        whole = act[window, :, :, 0:DEPTH].reshape((WIN + 2) * WIN, DEPTH)
        value = taps(sources, whole, WIN, w_one, tail_one) + shift_vec[0:1, :]
        inner[window] = value.reshape(WIN, WIN, C)
        keep_moments(window, value)
        return 0

    for step in range(CHUNKS, 2 * CHUNKS):
        run_act(step, 0)
    run_one(0, 0)
    run_one(1, 0)
    norm_lines(norm_two, line_of(gain_two), line_of(move_two))

    def merge(first, second, tap):
        main = first[:, 0:STRIDE] * cover[0, tap] + second[:, 0:STRIDE] * cover[1, tap]
        extra = first[:, 16:24] * wrap[tap]
        return jnp.concatenate([main[:, 0:8] + extra, main[:, 8:STRIDE]], axis=1)

    def store_pairs(target, at, count, parts):
        parts = [part.reshape(count, 2 * STRIDE, C) for part in parts]
        for place, part in enumerate(parts):
            target[at, :, place * MAIN : (place + 1) * MAIN] = part[:, :, 0:MAIN].astype(BF16)
        target[at, :, 3 * MAIN : DEPTH] = rests(parts)

    def run_merge(chunk, _):
        lines = []
        for window in range(2):
            value = inner[window, pl.ds(chunk * ROWS, ROWS)]
            value = activate(value, norm_two, window).astype(BF16).astype(F32)
            lines.append((pltpu.roll(value, 1, 1), value, pltpu.roll(value, WIN - 1, 1)))
        parts = [merge(lines[0][tap], lines[1][tap], tap) for tap in range(3)]
        at = pl.ds(chunk * (ROWS // 2), ROWS // 2)
        store_pairs(odd, at, ROWS // 2, parts)
        late = []
        for tap in range(3):
            late.append(jnp.concatenate([last[tap][None], parts[tap][0 : ROWS - 1]], axis=0))
            last[tap] = parts[tap][ROWS - 1]
            tops[chunk, tap] = parts[tap][0]
        store_pairs(even, at, ROWS // 2, late)
        return 0

    def merge_chunks(begin, end):
        if begin == 0:
            last[...] = jnp.zeros_like(last)
        lax.fori_loop(begin, end, run_merge, 0)
        if end == CHUNKS:
            lower = [jnp.zeros((1, STRIDE, C), F32)] * 3
        elif end in merged:
            lower = [tops[end, tap][None] for tap in range(3)]
        else:
            lower = None
        if lower is not None:
            ends = [jnp.concatenate([last[tap][None], lower[tap]], axis=0) for tap in range(3)]
            store_pairs(even, pl.ds(end * (ROWS // 2), 1), 1, ends)
        merged.update(range(begin, end))

    merged = set()

    for copy in copies_two:
        copy.wait()
    tails(w_two, tail_two)
    counted = cover[0, 1] + cover[1, 1]
    counted = jnp.concatenate([counted[0:8] + wrap[1], counted[8:STRIDE]], axis=0)

    def run_two(pair, count):
        def flat(source, at, number):
            return source[at : at + number, :, 0:DEPTH].reshape(number * 2 * STRIDE, DEPTH)

        sources = [flat(even, pair, count), flat(odd, pair, count), flat(even, pair + 1, count)]
        value = taps(sources, flat(even, pair, count + 1), STRIDE, w_two, tail_two)
        value = value.reshape(2 * count, STRIDE, C)
        at = slice(2 * pair, 2 * pair + 2 * count)
        first, second = start[0, at].astype(F32), start[1, at].astype(F32)
        value = value + merge(first, second, 1) + counted * line_of(conv_two_bias)
        band[front + 2 * pair : front + 2 * pair + 2 * count] = value

    def stage(target, base, begin, end):
        def one(pair, _):
            upper = band[base + 2 * pair]
            lower = band[base + 2 * pair + 1]
            target[pair] = jnp.concatenate([upper, lower], axis=0).astype(BF16)
            return 0

        lax.fori_loop(begin, end, one, 0)

    started = []

    def send(side, begin, end):
        if side == "prev":
            source, target, device = send_prev, from_next, (before, col)
            base = FRONT + 24 * lead - row_off - n_prev
        else:
            source, target, device = send_next, from_prev, (after, col)
            base = FRONT + 24 + 24 * lead - row_off
        stage(source, base, begin, end)
        place = len(started)
        copy = pltpu.make_async_remote_copy(
            src_ref=source.at[pl.ds(begin, end - begin)],
            dst_ref=target.at[pl.ds(begin, end - begin)],
            send_sem=out_send.at[place],
            recv_sem=out_recv.at[place],
            device_id=device,
            device_id_type=MESH,
        )
        copy.start()
        started.append(copy)

    for pair, count, begin, end, side, low, high in plan["first"]:
        merge_chunks(begin, end)
        run_two(pair, count)
        send(side, low, high)

    for pair, count, begin, end in plan["then"]:
        if end > begin:
            merge_chunks(begin, end)
        run_two(pair, count)
    for copy in started:
        copy.wait_recv()

    scale_cols = 1.0 / counted

    def finish(pair, has_prev, has_next):
        pieces = []
        for line in range(2):
            at = 2 * pair + line
            pieces.append(band[front + 24 * lead - row_off + at])
        value = jnp.concatenate(pieces, axis=0)
        if has_prev:
            value = value + from_prev[pair].astype(F32)
        if has_next:
            value = value + from_next[pair - (STRIDE - n_prev) // 2].astype(F32)
        for line in range(2):
            at = 2 * pair + line
            twice = lax.rem(at - row_off + 24, 24) < 8
            scale = jnp.where(twice, 0.5, 1.0)
            out_ref[at] = value[line * STRIDE : (line + 1) * STRIDE] * (scale_cols * scale)

    marks = sorted({0, n_next // 2, (STRIDE - n_prev) // 2, STRIDE // 2})
    for low, high in zip(marks[:-1], marks[1:]):
        has_prev = low < n_next // 2
        has_next = low >= (STRIDE - n_prev) // 2

        def one(pair, _, has_prev=has_prev, has_next=has_next):
            finish(pair, has_prev, has_next)
            return 0

        lax.fori_loop(low, high, one, 0)

    for copy in lat_copies + started:
        copy.wait_send()


def block_kernel(name, row_axis, ident, operands):
    plan = PLANS[name]
    hbm = pl.BlockSpec(memory_space=pl.ANY)
    vmem = pl.BlockSpec(memory_space=pltpu.VMEM)
    n_prev, n_next = max(plan["prev"], 2), max(plan["next"], 2)
    ext_rows = 56 if plan["lead"] else 40
    band_rows = FRONT + WIN + BACK
    scratch = [
        pltpu.SMEM((2,), jnp.int32),
        pltpu.SMEM((1,), jnp.int32),
        pltpu.VMEM((LATC, STRIDE, STRIDE), BF16),
        pltpu.VMEM((3, 3, LATC, C), BF16),
        pltpu.VMEM((2, ext_rows, 128), F32),
    ]
    scratch += [pltpu.VMEM((C,), F32)] * 8 + [pltpu.VMEM((TEMB,), F32)] * 2
    scratch += [
        pltpu.VMEM((C, TEMB), BF16),
        pltpu.VMEM((TEMB, TEMB), BF16),
        pltpu.VMEM((C, TEMB), BF16),
        pltpu.VMEM((3, DEPTH, C), BF16),
        pltpu.VMEM((3, DEPTH, C), BF16),
        pltpu.VMEM((DEPTH, 3 * REST), BF16),
        pltpu.VMEM((DEPTH, 3 * REST), BF16),
        pltpu.VMEM((128, C), BF16),
        pltpu.VMEM((2, WIN, MAIN), F32),
        pltpu.VMEM((2, 2, WIN, C), F32),
        pltpu.VMEM((2, 3, STRIDE, C), F32),
        pltpu.VMEM((3, 8, C), F32),
        pltpu.VMEM((C, C), BF16),
        pltpu.VMEM((8, C), F32),
        pltpu.VMEM((2, WIN + 2, WIN, 128), F32),
        pltpu.VMEM((2, WIN, WIN, C), BF16),
        pltpu.VMEM((2, WIN + 2, WIN, 4 * MAIN), BF16),
        pltpu.VMEM((2, WIN, WIN, C), F32),
        pltpu.VMEM((3, STRIDE, C), F32),
        pltpu.VMEM((CHUNKS, 3, STRIDE, C), F32),
        pltpu.VMEM((WIN // 2 + 1, 2 * STRIDE, 4 * MAIN), BF16),
        pltpu.VMEM((WIN // 2, 2 * STRIDE, 4 * MAIN), BF16),
        pltpu.VMEM((band_rows, STRIDE, C), F32),
        pltpu.VMEM((2, 8, C), F32),
        pltpu.VMEM((2, 8, C), F32),
        pltpu.VMEM((2, 2, 8, C), F32),
        pltpu.VMEM((2, 2, 8, C), F32),
        pltpu.VMEM((n_prev // 2, 2 * STRIDE, C), BF16),
        pltpu.VMEM((n_next // 2, 2 * STRIDE, C), BF16),
        pltpu.VMEM((n_next // 2, 2 * STRIDE, C), BF16),
        pltpu.VMEM((n_prev // 2, 2 * STRIDE, C), BF16),
        pltpu.SemaphoreType.DMA((4,)),
        pltpu.SemaphoreType.DMA((10,)),
        pltpu.SemaphoreType.DMA((3,)),
        pltpu.SemaphoreType.DMA((2, 18)),
        pltpu.SemaphoreType.DMA((5,)),
        pltpu.SemaphoreType.DMA((5,)),
        pltpu.SemaphoreType.DMA((3,)),
        pltpu.SemaphoreType.DMA((3,)),
    ]
    return pl.pallas_call(
        functools.partial(body, plan, row_axis),
        out_shape=jax.ShapeDtypeStruct((STRIDE, STRIDE, C), F32),
        in_specs=[hbm] * 19,
        out_specs=vmem,
        scratch_shapes=scratch,
        compiler_params=pltpu.CompilerParams(
            collective_id=ident, has_side_effects=True, vmem_limit_bytes=56 * 1024 * 1024
        ),
        cost_estimate=pl.CostEstimate(
            flops=3 * 2 * 1024 * 2880 * 320, bytes_accessed=10**7, transcendentals=10**6
        ),
        name="panorama_block",
    )(*operands)


def on_device(
    row_axis,
    latent,
    offsets,
    timestep,
    conv_in_weight,
    conv_in_bias,
    norm_one_gain,
    norm_one_shift,
    conv_one_weight,
    conv_one_bias,
    time_one_weight,
    time_one_bias,
    time_two_weight,
    time_two_bias,
    time_proj_weight,
    time_proj_bias,
    norm_two_gain,
    norm_two_shift,
    conv_two_weight,
    conv_two_bias,
):
    operands = (
        offsets,
        timestep,
        latent,
        conv_in_weight,
        conv_in_bias,
        norm_one_gain,
        norm_one_shift,
        conv_one_bias,
        time_proj_bias,
        norm_two_gain,
        norm_two_shift,
        conv_two_bias,
        time_one_bias,
        time_two_bias,
        conv_one_weight,
        conv_two_weight,
        time_one_weight,
        time_two_weight,
        time_proj_weight.T,
    )
    branches = [
        functools.partial(block_kernel, name, row_axis, place)
        for place, name in enumerate(("top", "mid", "low"))
    ]
    return lax.switch(2 - (((offsets[0] + 4) * 11) >> 7), branches, operands)


def solution(mesh):
    return jax.shard_map(
        functools.partial(on_device, mesh.shape["rows"]),
        mesh=mesh,
        in_specs=(P(None, "rows", "cols"),) + (P(),) * 18,
        out_specs=P("rows", "cols", None),
        check_vma=False,
    )
```
